256 devices in a mesh: ctx: 16 (over y_hi, x, core), fsdp: 16 (over y_lo, z).
Axes of the slice: x: 4, y: 4 (y_hi: 2, y_lo: 2; y = y_hi * 2 + y_lo), z: 8, core: 2. Of those that a mesh axis runs over, the one named last changes fastest.
Arguments:
- queries: bfloat16 [16, 256, 2048], P('fsdp', 'ctx'), may hold values from -8 to 8
- grad_out: bfloat16 [16, 256, 2048], P('fsdp', 'ctx'), may hold values from -384 to 384
- keys: bfloat16 [16, 4096, 2048], P('fsdp', 'ctx'), may hold values from -8 to 8
- context: bfloat16 [16, 4096, 2048], P('fsdp', 'ctx'), may hold values from -6 to 6
- value_weight: bfloat16 [2048, 2048], P('fsdp'), may hold values from -0.125 to 0.125
- plan: int32 [16, 2, 2], P('fsdp'), may hold values from 0 to 12, as said below
- lengths: int32 [16, 2], P('fsdp'), may hold values from 128 to 3072, as said below
- blocks: int32 [16, 64], P('fsdp', 'ctx'), may hold values from -1 to 47, as said below
Outputs:
- query_grad: bfloat16 [16, 256, 2048], P('fsdp', 'ctx')
- key_grad: bfloat16 [16, 4096, 2048], P('fsdp', 'ctx')
- context_grad: bfloat16 [16, 4096, 2048], P('fsdp', 'ctx')
- weight_grad: float32 [2048, 2048], P(('ctx', 'fsdp'))
The draws below stay inside these ranges and needn't reach their ends.
Inputs may be any that keep to these rules, and one draw needn't show every extreme that they name: plan[f, 0, e] is the first context index of episode e's group and plan[f, 1, e] its width; the groups of a replica are contiguous, in order, and cover all 16 indices; every width is 4 or more. `lengths`: an episode's length is at most 256 times its group's width; in every replica the episode of the wider group has exactly that length. Each slot of 64 keys holds -1 if it is empty, else the number b of the block of its group's episode that it holds, keys b * 64 to b * 64 + 63 of the episode; the blocks 0 to ceil(length / 64) - 1 of each episode are held exactly once, by slots of its group, and its group's other slots are -1.
All inputs are finite; a program needn't handle non-finite values.
Results may differ from the reference program's by a relative error of at most 0.034.
Values may be sent and summed in bfloat16 or wider, within the bound.
No kernel may reach another device: no remote copies, remote signals or barrier semaphores. Data moves between devices by JAX's collectives and lax.ppermute only.
A program may use at most 128 MiB of HBM per device.

```python
import math
import jax
import jax.numpy as jnp
from jax import lax

D = 2048
HEADS = 16
HD = 128
HQ = 2048
QC = 128
EPS = 2
BLK = 64
KB_DEV = 256
SLOTS_DEV = 4
N_CTX = 16
N_FSDP = 16


def episode_plan(key):
    width_key = jax.random.fold_in(key, 0)
    length_key = jax.random.fold_in(key, 1)
    score_key = jax.random.fold_in(key, 3)
    lowest = N_CTX // 4
    coin = jax.random.randint(width_key, (N_FSDP,), 0, 2).astype(jnp.int32)
    first = jnp.where(coin == 0, lowest, N_CTX - lowest).astype(jnp.int32)
    widths = jnp.stack([first, N_CTX - first], axis=1).astype(jnp.int32)
    starts = jnp.stack([jnp.zeros_like(first), first], axis=1).astype(jnp.int32)
    capacity = widths * KB_DEV
    raw_draw = jax.random.randint(length_key, (N_FSDP, 2), 0, 1 << 30).astype(jnp.int32)
    episode_len = QC + raw_draw % (capacity - QC + 1)
    full_one = (first * 2 < N_CTX).astype(jnp.int32)
    pick = jnp.arange(2, dtype=jnp.int32)[None, :] == full_one[:, None]
    episode_len = jnp.where(pick, capacity, episode_len).astype(jnp.int32)
    slot_total = N_CTX * SLOTS_DEV
    slot_ids = jnp.arange(slot_total, dtype=jnp.int32)
    slot_device = slot_ids // SLOTS_DEV
    slot_episode = (slot_device[None, :] >= first[:, None]).astype(jnp.int32)
    random_rank = jax.random.randint(score_key, (N_FSDP, slot_total), 0, 1 << 16).astype(jnp.int32)
    keyed = slot_episode * (1 << 26) + random_rank * slot_total + slot_ids[None, :]
    sorted_slots = jnp.argsort(keyed, axis=1).astype(jnp.int32)
    placing = jnp.argsort(sorted_slots, axis=1).astype(jnp.int32)
    in_group = placing - slot_episode * first[:, None] * SLOTS_DEV
    needed = (episode_len + BLK - 1) // BLK
    slot_need = jnp.where(slot_episode == 0, needed[:, 0:1], needed[:, 1:2])
    held = jnp.where(in_group < slot_need, in_group, -1).astype(jnp.int32)
    return (starts, widths, episode_len, held)


def draw_queries(key, part):
    key = jax.random.fold_in(key, 5)
    noise_key = jax.random.fold_in(key, 0)
    samples = jax.random.normal(noise_key, (N_FSDP, EPS * QC, HQ), jnp.float32)
    return jnp.clip(samples, -8.0, 8.0).astype(jnp.bfloat16)


def draw_keys(key, part):
    key = jax.random.fold_in(key, 7)
    noise_key = jax.random.fold_in(key, 0)
    samples = jax.random.normal(noise_key, (N_FSDP, N_CTX * KB_DEV, HQ), jnp.float32)
    return jnp.clip(samples, -8.0, 8.0).astype(jnp.bfloat16)


def draw_plan(key, part):
    starts, widths, episode_len, held = episode_plan(key)
    return jnp.stack([starts, widths], axis=1).astype(jnp.int32)


def draw_lengths(key, part):
    starts, widths, episode_len, held = episode_plan(key)
    return episode_len


def draw_blocks(key, part):
    starts, widths, episode_len, held = episode_plan(key)
    return held


def strengthened(result, stream_key, source, target, shards_of, factor):
    def block_of(axis_at):
        return (jnp.arange(result.shape[axis_at]) // (result.shape[axis_at] // shards_of)).reshape((-1,) + (1,) * (result.ndim - 1 - axis_at))

    near = jax.random.permutation(stream_key, shards_of)[block_of(target)]
    second = (block_of(target) + shards_of // 2) % shards_of
    return jnp.where((block_of(source) == near) | (block_of(source) == second), factor * result, result)


def shard_levels(own_key, dims, cuts, low, top_value):
    level = 1.0
    for position, blocks in cuts:
        draws = jax.random.uniform(jax.random.fold_in(jax.random.fold_in(own_key, 6), position), (blocks,), jnp.float32, low / len(cuts), top_value / len(cuts))
        level = level * jnp.repeat(jnp.exp(draws), dims[position] // blocks).reshape((-1,) + (1,) * (len(dims) - 1 - position))
    return level


def bell_draw(key, dims, spread, bound, cuts=(), kind=jnp.bfloat16):
    array = spread * jax.random.normal(key, dims, jnp.float32)
    if cuts:
        array = array * shard_levels(key, dims, cuts, -0.22, 0.18)
    return jnp.clip(array, -bound, bound).astype(kind)


def gaussian_with(key, extent, deviation, limit, cuts, heavy, kind=jnp.bfloat16):
    values = deviation * jax.random.normal(key, extent, jnp.float32)
    if cuts:
        values = values * shard_levels(key, extent, cuts, -0.22, 0.18)
    return jnp.clip(strengthened(values, jax.random.fold_in(key, 3), *heavy), -limit, limit).astype(kind)


def setup_inputs(seed: int = 0) -> dict:
    key_of = jax.random.split(jax.random.key(seed), 9)
    return {
        "queries": draw_queries(jax.random.fold_in(key_of[8], 71), 0),
        "grad_out": bell_draw(key_of[1], (N_FSDP, EPS * QC, HQ), 64.0, 384.0, ((0, 16), (1, 16))),
        "keys": draw_keys(jax.random.fold_in(key_of[8], 71), 0),
        "context": gaussian_with(key_of[3], (N_FSDP, N_CTX * KB_DEV, D), 1.0, 6.0, ((0, 16), (1, 16)), (1, 2, 16, 2.0)),
        "value_weight": bell_draw(key_of[4], (D, HQ), D ** -0.5, 0.125, ((0, 16),)),
        "plan": draw_plan(jax.random.fold_in(key_of[8], 71), 0),
        "lengths": draw_lengths(jax.random.fold_in(key_of[8], 71), 0),
        "blocks": draw_blocks(jax.random.fold_in(key_of[8], 71), 0),
    }


neg_large = -1e+30

def replica_grads(queries, grad_out, keys, context, weight, plan_row, length_row, block_row):
    query_rows = EPS * QC
    kv_rows = N_CTX * KB_DEV
    score_scale = 1.0 / math.sqrt(HD)
    values = jnp.dot(context, weight, preferred_element_type=jnp.float32).astype(jnp.bfloat16)
    starts = plan_row[0]
    widths = plan_row[1]
    key_ids = jnp.arange(kv_rows, dtype=jnp.int32)
    device_of = key_ids // KB_DEV
    numbers = jnp.arange(EPS, dtype=jnp.int32)
    member = (device_of[:, None] >= starts[None, :]) & (device_of[:, None] < (starts + widths)[None, :])
    key_episode = lax.optimization_barrier(jnp.sum(jnp.where(member, numbers[None, :], 0), axis=1)).astype(jnp.int32)
    block_of = block_row[key_ids // BLK]
    key_pos = block_of * BLK + key_ids % BLK
    key_live = (block_of >= 0) & (key_pos < length_row[key_episode])
    row_ids = jnp.arange(query_rows, dtype=jnp.int32)
    query_episode = row_ids // QC
    query_pos = length_row[query_episode] - QC + row_ids % QC
    allowed = (query_episode[:, None] == key_episode[None, :]) & key_live[None, :] & (key_pos[None, :] <= query_pos[:, None])
    visible = allowed[None, :, :]
    query_f = queries.astype(jnp.float32).reshape(query_rows, HEADS, HD)
    grad_f = grad_out.astype(jnp.float32).reshape(query_rows, HEADS, HD)
    key_f = keys.astype(jnp.float32).reshape(kv_rows, HEADS, HD)
    value_f = values.astype(jnp.float32).reshape(kv_rows, HEADS, HD)
    scores = jnp.einsum('qhd,khd->hqk', query_f, key_f) * score_scale
    masked = jnp.where(visible, scores, neg_large)
    row_max = lax.optimization_barrier(jnp.max(masked, axis=-1, keepdims=True))
    raw = jnp.where(visible, jnp.exp(scores - row_max), 0.0)
    probs = raw / lax.optimization_barrier(jnp.sum(raw, axis=-1, keepdims=True))
    prods = jnp.einsum('qhd,khd->hqk', grad_f, value_f)
    row_delta = lax.optimization_barrier(jnp.sum(probs * prods, axis=-1, keepdims=True))
    dscore = probs * (prods - row_delta)
    probs_b = lax.optimization_barrier(probs.astype(jnp.bfloat16)).astype(jnp.float32)
    dscore_b = lax.optimization_barrier(dscore.astype(jnp.bfloat16)).astype(jnp.float32)
    value_grad = jnp.einsum('hqk,qhd->khd', probs_b, grad_f).reshape(kv_rows, HQ).astype(jnp.bfloat16)
    key_grad = (score_scale * jnp.einsum('hqk,qhd->khd', dscore_b, query_f)).reshape(kv_rows, HQ).astype(jnp.bfloat16)
    query_grad = (score_scale * jnp.einsum('hqk,khd->qhd', dscore_b, key_f)).reshape(query_rows, HQ).astype(jnp.bfloat16)
    context_grad = jnp.dot(value_grad, weight.T, preferred_element_type=jnp.float32).astype(jnp.bfloat16)
    partial_grad = jnp.dot(context.T, value_grad, preferred_element_type=jnp.float32)
    return (query_grad, key_grad, context_grad, partial_grad)

def reference(queries, grad_out, keys, context, value_weight, plan, lengths, blocks):

    def one_replica(running, pieces):
        query_in, grad_in, key_in, context_in, plan_in, length_in, block_in = pieces
        query_out, key_out, context_out, partial_grad = replica_grads(query_in, grad_in, key_in, context_in, value_weight, plan_in, length_in, block_in)
        return (running + partial_grad, (query_out, key_out, context_out))
    start_sum = jnp.zeros((D, HQ), jnp.float32)
    grad_sum, outputs = lax.scan(one_replica, start_sum, (queries, grad_out, keys, context, plan, lengths, blocks))
    return (outputs[0], outputs[1], outputs[2], grad_sum)
```

```python
import functools
import math

import jax
import jax.numpy as jnp
from jax import lax
from jax.experimental import pallas as pl
from jax.experimental.pallas import tpu as pltpu
from jax.sharding import Mesh, PartitionSpec as P

HD = 128
QC = 128
HEADS = 16
BLK = 64
TOK = 256
WIDTH = 2048
SCALE = 1.0 / math.sqrt(HD)
NEG = -1e30
BF = jnp.bfloat16
F32 = jnp.float32
CTX = ("yh", "x", "k")
AXES = ("yh", "x", "k", "yl", "z")
VMEM = pl.BlockSpec(memory_space=pltpu.VMEM)
SMEM = pl.BlockSpec(memory_space=pltpu.SMEM)

I_X, I_K, I_YH, I_EP, I_S0, I_W0, I_S1, I_W1, I_LEN, I_BLK = range(10)


def params(megabytes):
    return pltpu.CompilerParams(vmem_limit_bytes=megabytes << 20)


def cost(flops, size):
    return pl.CostEstimate(flops=flops, bytes_accessed=size, transcendentals=0)


def dot(a, b, ca, cb):
    return lax.dot_general(a, b, (((ca,), (cb,)), ((), ())), preferred_element_type=F32)


def shift(a, axis, by):
    n = lax.axis_size(axis)
    return lax.ppermute(a, axis, [(i, (i + by) % n) for i in range(n)])


def own_rows(qg_ref, which, episode, dst):
    for i in range(8):
        dst[i * 16 : (i + 1) * 16, :] = qg_ref[8 * episode + i, which]


def scores_kernel(info, qg_ref, k_ref, p0, p1, p2, p3, st_ref, q_buf):
    episode = info[I_EP]
    own_rows(qg_ref, 0, episode, q_buf)
    length = info[I_LEN]
    row = lax.broadcasted_iota(jnp.int32, (BLK, QC), 0)
    col = lax.broadcasted_iota(jnp.int32, (BLK, QC), 1)
    limit = jnp.minimum(length - QC + col, length - 1)
    masks = []
    for slot in range(TOK // BLK):
        b = info[I_BLK + slot]
        pos = b * BLK + row
        masks.append((pos <= limit) & (b >= 0))
    visible = jnp.concatenate(masks, axis=0)
    for s, out in enumerate((p0, p1, p2, p3)):
        block = lax.rem(info[I_X] + s, 4)
        for hh in range(4):
            cols = pl.ds(pl.multiple_of(block * 512 + hh * HD, HD), HD)
            sc = dot(k_ref[:, cols], q_buf[:, cols], 1, 1) * SCALE
            masked = jnp.where(visible, sc, NEG)
            top = jnp.max(masked, axis=0, keepdims=True)
            p = jnp.where(visible, jnp.exp(masked - top), 0.0)
            st_ref[0, block, hh : hh + 1, :] = top
            st_ref[1, block, hh : hh + 1, :] = jnp.sum(p, axis=0, keepdims=True)
            out[:, hh * HD : (hh + 1) * HD] = p.astype(BF)


def member(info, ctx_index, e):
    start = info[I_S0 + 2 * e]
    return (ctx_index >= start) & (ctx_index < start + info[I_W0 + 2 * e])


def totals(info, st_ref, e, block):
    top = jnp.full((4, QC), NEG, F32)
    for c in range(16):
        top = jnp.maximum(top, jnp.where(member(info, c, e), st_ref[c, 0, block], NEG))
    total = jnp.zeros((4, QC), F32)
    for c in range(16):
        part = st_ref[c, 1, block] * jnp.exp(st_ref[c, 0, block] - top)
        total = total + jnp.where(member(info, c, e), part, 0.0)
    return top, 1.0 / total


def block_kernel(info, st_ref, qg_ref, *refs):
    p_refs, c_refs = refs[:8], refs[8:16]
    out_ref, g_buf, vg_buf = refs[16:]
    xi = info[I_X]
    cols = pl.ds(pl.multiple_of(xi * 512, 512), 512)
    tops, invs = [], []
    for e in range(2):
        for i in range(8):
            g_buf[e, i * 16 : (i + 1) * 16, :] = qg_ref[8 * e + i, 1, :, cols]
        top, inv = totals(info, st_ref, e, xi)
        tops.append(top)
        invs.append(inv)
    for n in range(8):
        src_x = lax.rem(xi + 4 - n // 2, 4)
        src_k = info[I_K] if n % 2 == 0 else 1 - info[I_K]
        c = info[I_YH] * 8 + src_x * 2 + src_k
        in_one = member(info, c, 1)
        top = jnp.where(in_one, tops[1], tops[0])
        inv = jnp.where(in_one, invs[1], invs[0])
        factor = jnp.exp(st_ref[c, 0, xi] - top) * inv
        e = in_one.astype(jnp.int32)
        for hh in range(4):
            hs = slice(hh * HD, (hh + 1) * HD)
            pr = (p_refs[n][:, hs].astype(F32) * factor[hh : hh + 1, :]).astype(BF)
            vg_buf[n * TOK : (n + 1) * TOK, hs] = dot(pr, g_buf[e, :, hs], 1, 0).astype(BF)
    for tile in range(4):
        acc = jnp.zeros((256, 512), F32)
        for n in range(8):
            acc = acc + dot(
                c_refs[n][:, tile * 256 : (tile + 1) * 256],
                vg_buf[n * TOK : (n + 1) * TOK, :],
                0,
                0,
            )
        for part in range(4):
            r = tile * 256 + part * 64
            yh, xx, yl = r // 512, (r // 128) % 4, (r // 64) % 2
            out_ref[yh * 2 + yl, xx] = acc[part * 64 : (part + 1) * 64].astype(BF)


def values_kernel(
    info, st_ref, qg_ref, ctx_ref, wa, wb, p0, p1, p2, p3,
    prod_ref, probs_ref, cross_ref, cg_ref, g_buf, v_buf, vg_buf,
):
    episode = info[I_EP]
    xi = info[I_X]
    ki = info[I_K]
    own_rows(qg_ref, 1, episode, g_buf)
    col_a = pl.ds(pl.multiple_of(ki * 1024, 1024), 1024)
    col_b = pl.ds(pl.multiple_of((1 - ki) * 1024, 1024), 1024)
    ca, cb = ctx_ref[:, col_a], ctx_ref[:, col_b]
    for t in range(4):
        ts = slice(t * 512, (t + 1) * 512)
        v_buf[:, ts] = (dot(ca, wa[:, ts], 1, 0) + dot(cb, wb[:, ts], 1, 0)).astype(BF)
    me = info[I_YH] * 8 + xi * 2 + ki
    for s, p_ref in enumerate((p0, p1, p2, p3)):
        block = lax.rem(xi + s, 4)
        top, inv = totals(info, st_ref, episode, block)
        factor = jnp.exp(st_ref[me, 0, block] - top) * inv
        for hh in range(4):
            cols = pl.ds(pl.multiple_of(block * 512 + hh * HD, HD), HD)
            pr = p_ref[:, hh * HD : (hh + 1) * HD].astype(F32) * factor[hh : hh + 1, :]
            prod = dot(v_buf[:, cols], g_buf[:, cols], 1, 1)
            prod_ref[:, cols] = prod
            probs_ref[:, cols] = pr
            cross_ref[block, hh : hh + 1, :] = jnp.sum(pr * prod, axis=0, keepdims=True)
            vg_buf[:, cols] = dot(pr.astype(BF), g_buf[:, cols], 1, 0).astype(BF)
    vg = vg_buf[...]
    for w_ref, base in ((wa, ki * 1024), (wb, (1 - ki) * 1024)):
        for t in range(2):
            dst = pl.ds(pl.multiple_of(base + t * 512, 512), 512)
            cg_ref[:, dst] = dot(vg, w_ref[t * 512 : (t + 1) * 512, :], 1, 1).astype(BF)


def grads_kernel(info, cross_ref, qg_ref, k_ref, prod_ref, probs_ref, kg_ref, qp_ref, q_buf):
    episode = info[I_EP]
    own_rows(qg_ref, 0, episode, q_buf)
    for i in range(8):
        qp_ref[1 - episode, i] = jnp.zeros((16, WIDTH), BF)
    for block in range(4):
        delta = jnp.zeros((4, QC), F32)
        for c in range(16):
            delta = delta + jnp.where(member(info, c, episode), cross_ref[c, block], 0.0)
        for hh in range(4):
            hs = slice(block * 512 + hh * HD, block * 512 + (hh + 1) * HD)
            ds = (probs_ref[:, hs] * (prod_ref[:, hs] - delta[hh : hh + 1, :])).astype(BF)
            kg_ref[:, hs] = (SCALE * dot(ds, q_buf[:, hs], 1, 0)).astype(BF)
            part = (SCALE * dot(ds, k_ref[:, hs], 0, 0)).astype(BF)
            for i in range(8):
                qp_ref[episode, i, :, hs] = part[i * 16 : (i + 1) * 16]


def on_device(queries, grad_out, keys, context, value_weight, plan, lengths, blocks):
    yh, xi, ki, yl, zi = (lax.axis_index(a) for a in AXES)
    my_index = yh * 8 + xi * 2 + ki
    keys, context = keys[0], context[0]
    in_one = (my_index >= plan[0, 0, 1]) & (my_index < plan[0, 0, 1] + plan[0, 1, 1])
    episode = in_one.astype(jnp.int32)
    own_length = jnp.where(in_one, lengths[0, 1], lengths[0, 0])
    info = jnp.concatenate([
        jnp.stack([
            xi, ki, yh, episode, plan[0, 0, 0], plan[0, 1, 0], plan[0, 0, 1], plan[0, 1, 1], own_length
        ]).astype(jnp.int32),
        blocks[0],
    ])

    qg = jnp.concatenate([queries, grad_out], axis=0)
    qg_all = lax.all_to_all(jnp.broadcast_to(qg[None], (16,) + qg.shape), CTX, 0, 0)

    w_own = value_weight
    place = lambda y, k: ((y // 2) * 2 + k) * 2 + y % 2
    owners = [(y, k) for y in range(4) for k in range(2) if y % 2 == k]
    around = ("yh", "k", "yl")
    top = lax.ppermute(w_own[:64], around, [(place(y, k), place((y + 1) % 4, k)) for y, k in owners])
    bot = lax.ppermute(w_own[64:], around, [(place(y, k), place((y + 3) % 4, k)) for y, k in owners])
    w_mine = jnp.where(yl == ki, w_own, jnp.concatenate([top, bot], axis=0))
    w_a = lax.all_gather(w_mine, "z", axis=0, tiled=True)
    w_b = shift(w_a, "k", 1)

    cv = context.reshape(TOK, 8, 2, 128)
    c_mine = jnp.where(ki == 0, cv[:, :, 0], cv[:, :, 1]).reshape(TOK, 1024)
    c_oth = jnp.where(ki == 0, cv[:, :, 1], cv[:, :, 0]).reshape(TOK, 1024)
    c_part = shift(c_oth, "k", 1)
    c_m1, c_p1 = shift(c_mine, "x", 1), shift(c_mine, "x", -1)
    d_m1, d_p1 = shift(c_part, "x", 1), shift(c_part, "x", -1)
    c_2 = shift(c_m1, "x", 1)
    d_2 = shift(d_p1, "x", -1)

    sd = jax.ShapeDtypeStruct
    p0, p1, p2, p3, st = pl.pallas_call(
        scores_kernel,
        in_specs=[SMEM, VMEM, VMEM],
        out_specs=[VMEM] * 5,
        out_shape=[sd((TOK, 512), BF)] * 4 + [sd((2, 4, 4, QC), F32)],
        scratch_shapes=[pltpu.VMEM((QC, WIDTH), BF)],
        compiler_params=params(32),
        cost_estimate=cost(134 << 20, 4 << 20),
        name="scores",
    )(info, qg_all, keys)

    p_m1, p_p1, p_2 = shift(p1, "x", 1), shift(p3, "x", -1), shift(p2, "x", 2)
    st_all = lax.all_to_all(jnp.broadcast_to(st[None], (16,) + st.shape), CTX, 0, 0)
    r_0, r_m1, r_p1, r_2 = (shift(a, "k", 1) for a in (p0, p_m1, p_p1, p_2))

    pieces = pl.pallas_call(
        block_kernel,
        in_specs=[SMEM] + [VMEM] * 18,
        out_specs=VMEM,
        out_shape=sd((4, 4, 64, 512), BF),
        scratch_shapes=[pltpu.VMEM((2, QC, 512), BF), pltpu.VMEM((8 * TOK, 512), BF)],
        compiler_params=params(40),
        cost_estimate=cost(2400 << 20, 10 << 20),
        name="block_grad",
    )(
        info, st_all, qg_all,
        p0, r_0, p_m1, r_m1, p_2, r_2, p_p1, r_p1,
        c_mine, c_part, c_m1, d_m1, c_2, d_2, c_p1, d_p1,
    )

    got = lax.all_to_all(pieces, ("yh", "yl"), 0, 0)
    summed = jnp.sum(got.astype(F32), axis=0).reshape(4, 8, 8, 512)
    z_in = summed.transpose(1, 0, 2, 3).astype(BF).reshape(8, 32, 512)
    z_out = lax.all_to_all(z_in, "z", 0, 0)
    x_in = jnp.sum(z_out.astype(F32), axis=0).reshape(4, 8, 512)
    x_out = lax.all_to_all(x_in, "x", 0, 0)
    weight_grad = x_out.transpose(1, 0, 2).reshape(8, WIDTH)

    prods, probs, cross, context_grad = pl.pallas_call(
        values_kernel,
        in_specs=[SMEM] + [VMEM] * 9,
        out_specs=[VMEM] * 4,
        out_shape=[sd((TOK, WIDTH), F32), sd((TOK, WIDTH), F32), sd((4, 4, QC), F32), sd((TOK, WIDTH), BF)],
        scratch_shapes=[pltpu.VMEM((QC, WIDTH), BF), pltpu.VMEM((TOK, WIDTH), BF), pltpu.VMEM((TOK, WIDTH), BF)],
        compiler_params=params(48),
        cost_estimate=cost(4600 << 20, 16 << 20),
        name="values",
    )(info, st_all, qg_all, context, w_a, w_b, p0, p1, p2, p3)

    cross_all = lax.all_to_all(jnp.broadcast_to(cross[None], (16,) + cross.shape), CTX, 0, 0)

    key_grad, q_part = pl.pallas_call(
        grads_kernel,
        in_specs=[SMEM] + [VMEM] * 5,
        out_specs=[VMEM] * 2,
        out_shape=[sd((TOK, WIDTH), BF), sd((2, 8, 16, WIDTH), BF)],
        scratch_shapes=[pltpu.VMEM((QC, WIDTH), BF)],
        compiler_params=params(40),
        cost_estimate=cost(270 << 20, 8 << 20),
        name="grads",
    )(info, cross_all, qg_all, keys, prods, probs)

    q_got = lax.all_to_all(q_part.reshape(16, 16, WIDTH), CTX, 0, 0)
    query_grad = jnp.sum(q_got.astype(F32), axis=0).astype(BF)
    return (query_grad[None], key_grad[None], context_grad[None], weight_grad)


def solution(mesh):
    fine = Mesh(mesh.devices.reshape(2, 4, 2, 2, 8), AXES)
    fsdp = ("yl", "z")
    rows = P(fsdp, CTX, None)
    return jax.shard_map(
        on_device,
        mesh=fine,
        in_specs=(rows, rows, rows, rows, P(fsdp, None), P(fsdp, None, None), P(fsdp, None), P(fsdp, CTX)),
        out_specs=(rows, rows, rows, P(AXES, None)),
        check_vma=False,
    )
```

```python
import functools
import math

import jax
import jax.numpy as jnp
from jax import lax
from jax.experimental import pallas as pl
from jax.experimental.pallas import tpu as pltpu
from jax.sharding import Mesh, PartitionSpec as P

HD = 128
QC = 128
HEADS = 16
BLK = 64
TOK = 256
WIDTH = 2048
SCALE = 1.0 / math.sqrt(HD)
NEG = -1e30
BF = jnp.bfloat16
F32 = jnp.float32
CTX = ("yh", "x", "k")
AXES = ("yh", "x", "k", "yl", "z")
VMEM = pl.BlockSpec(memory_space=pltpu.VMEM)
SMEM = pl.BlockSpec(memory_space=pltpu.SMEM)

BLOCK = 512
SOURCE_STEP = (0, 3, 1, 2)

def params(megabytes):
    return pltpu.CompilerParams(vmem_limit_bytes=megabytes << 20)


def cost(flops, size):
    return pl.CostEstimate(flops=flops, bytes_accessed=size, transcendentals=0)


def dot(a, b, ca, cb):
    return lax.dot_general(a, b, (((ca,), (cb,)), ((), ())), preferred_element_type=F32)


def shift(a, axis, by):
    n = lax.axis_size(axis)
    return lax.ppermute(a, axis, [(i, (i + by) % n) for i in range(n)])


class Info:
    def __init__(self, plan, lengths, blocks):
        self.x, self.k, self.yh, self.yl = (lax.axis_index(a) for a in ("x", "k", "yh", "yl"))
        self.start, self.width = plan[0, 0, 1], plan[0, 1, 1]
        self.lengths = [lengths[0, e] for e in range(2)]
        self.blocks = blocks


class Fetched:
    def __init__(self, src, dst, sem):
        self.copy = pltpu.make_async_copy(src, dst, sem)
        self.ref = dst
        self.copy.start()
        self.pending = True

    def __getitem__(self, at):
        self.ready()
        return self.ref[at]

    def ready(self):
        if self.pending:
            self.copy.wait()
            self.pending = False


def call(scalars, kernel, name, outs, args, flops, size, scratch=(), ties=(), picks=None, megabytes=48):
    n_in, n_out, n_tie = len(args), len(outs), len(ties)
    picks = picks or {}

    def body(plan, lengths, blocks, *refs):
        info = Info(plan, lengths, blocks)
        srcs, refs = refs[:n_in], refs[n_in + n_tie :]
        out_refs, refs = refs[:n_out], refs[n_out + n_tie :]
        bufs, sems, rest = refs[:n_in], refs[n_in], refs[n_in + 1 :]
        srcs = [picks[i][0](info, a) if i in picks else a for i, a in enumerate(srcs)]
        ins = [Fetched(a, b, sems.at[i]) for i, (a, b) in enumerate(zip(srcs, bufs))]
        kernel(info, *ins, *out_refs, *rest)
        for a in ins:
            a.ready()

    anywhere = pl.BlockSpec(memory_space=pl.ANY)
    return pl.pallas_call(
        body,
        in_specs=[SMEM] * 3 + [anywhere] * (n_in + n_tie),
        out_specs=[VMEM] * n_out + [anywhere] * n_tie,
        out_shape=[jax.ShapeDtypeStruct(shape, kind) for shape, kind in outs]
        + [jax.ShapeDtypeStruct(a.shape, a.dtype) for a in ties],
        scratch_shapes=[
            pltpu.VMEM(picks[i][1] if i in picks else a.shape, a.dtype) for i, a in enumerate(args)
        ]
        + [pltpu.SemaphoreType.DMA((n_in,))]
        + [pltpu.VMEM(shape, kind) for shape, kind in scratch],
        input_output_aliases={3 + n_in + i: n_out + i for i in range(n_tie)},
        compiler_params=params(megabytes),
        cost_estimate=cost(1, 1),
        name=name,
    )(*scalars, *args, *ties)


def source(info, n):
    sx = lax.rem(info.x + SOURCE_STEP[n], 4)
    c = info.yh * 8 + sx * 2 + info.k
    return sx, (c >= info.start) & (c < info.start + info.width)


def pack_kernel(info, k_ref, q_ref, g_ref, w_ref, out_ref, w_out):
    for b in range(4):
        at = pl.ds(pl.multiple_of(b * BLOCK + info.k * 256, 256), 256)
        w_out[:, b * 256 : (b + 1) * 256] = w_ref[:, at]
    row = lax.broadcasted_iota(jnp.int32, (16, BLOCK), 0)
    held = jnp.zeros((16, BLOCK), F32)
    for slot in range(TOK // BLK):
        held = jnp.where(row == slot, info.blocks[0, slot].astype(F32), held)
    for x in range(4):
        cols = slice(x * BLOCK, (x + 1) * BLOCK)
        out_ref[x, 256:272, :] = q_ref[:, cols]
        out_ref[x, 272:288, :] = g_ref[:, cols]
        out_ref[x, 288:304, :] = held.astype(BF)
        out_ref[x, 0:256, :] = k_ref[:, cols]


def unpack_kernel(info, pay, out_ref):
    for i in range(4):
        out_ref[i] = pay[i]


def gather_rows(info, own, pay_k, pay_y, pay_ky, qg_ref):
    ki, yh = info.k, info.yh
    for pay, base, e, k in (
        (own, 256, yh, ki), (pay_k, 0, yh, 1 - ki), (pay_y, 0, 1 - yh, ki), (pay_ky, 0, 1 - yh, 1 - ki),
    ):
        for which in range(2):
            for i in range(4):
                at = pl.ds(pl.multiple_of((i * 2 + k) * 16, 16), 16)
                lo = base + which * 16
                qg_ref[which, e, at, :] = pay[i, lo : lo + 16, :]


def scores_kernel(info, own, pay_k, pay_y, pay_ky, p_ref, top_ref, ex_ref, qg_ref):
    gather_rows(info, own, pay_k, pay_y, pay_ky, qg_ref)
    row = lax.broadcasted_iota(jnp.int32, (BLK, QC), 0).astype(F32)
    col = lax.broadcasted_iota(jnp.int32, (BLK, QC), 1).astype(F32)
    tops, sums, ones = [], [], []
    for n in range(4):
        sx, in_one = source(info, n)
        e = in_one.astype(jnp.int32)
        length = jnp.where(in_one, info.lengths[1], info.lengths[0]).astype(F32)
        held = own[sx, 288:304, 0:QC].astype(F32)
        masks = []
        for slot in range(TOK // BLK):
            b = held[slot : slot + 1, :]
            masks.append((b >= 0.0) & (b * BLK + row <= length - QC + col))
        visible = jnp.concatenate(masks, axis=0)
        top_rows, sum_rows = [], []
        for hh in range(4):
            hs = slice(hh * HD, (hh + 1) * HD)
            masked = jnp.where(visible, dot(own[sx, 0:256, hs], qg_ref[0, e, :, hs], 1, 1) * SCALE, NEG)
            top = jnp.max(masked, axis=0, keepdims=True)
            p = jnp.where(visible, jnp.exp(masked - top), 0.0)
            p_ref[n, :, hs] = p
            top_rows.append(top)
            sum_rows.append(jnp.sum(p, axis=0, keepdims=True))
        tops.append(jnp.concatenate(top_rows, axis=0))
        sums.append(jnp.concatenate(sum_rows, axis=0))
        ones.append(in_one)
        top_ref[n] = tops[n]
    for e in range(2):
        of_e = [one if e else jnp.logical_not(one) for one in ones]
        top = jnp.full((4, QC), NEG, F32)
        for n in range(4):
            top = jnp.maximum(top, jnp.where(of_e[n], tops[n], NEG))
        total = jnp.zeros((4, QC), F32)
        for n in range(4):
            total = total + jnp.where(of_e[n], sums[n] * jnp.exp(tops[n] - top), 0.0)
        ex_ref[0, e] = top
        ex_ref[1, e] = total


def probs_kernel(
    info, qg_ref, p_ref, top_ref, x0, x1, x2, x3, v0, v1, v2, v3, u1, u2, u3, fac_ref
):
    tops, invs = [], []
    for e in range(2):
        top = jnp.maximum(
            jnp.maximum(x0[0, e], x1[0, e]), jnp.maximum(x2[0, e], x3[0, e])
        )
        total = jnp.zeros((4, QC), F32)
        for x_ref in (x0, x1, x2, x3):
            total = total + x_ref[1, e] * jnp.exp(x_ref[0, e] - top)
        tops.append(top)
        invs.append(1.0 / total)
    for n, home in enumerate(((v0,), (v1, u1), (v2, u2), (v3, u3))):
        _, in_one = source(info, n)
        e = in_one.astype(jnp.int32)
        top = jnp.where(in_one, tops[1], tops[0])
        factor = jnp.exp(top_ref[n] - top) * jnp.where(in_one, invs[1], invs[0])
        fac_ref[n] = factor
        for hh in range(4):
            hs = slice(hh * HD, (hh + 1) * HD)
            pr = (p_ref[n, :, hs] * factor[hh : hh + 1, :]).astype(BF)
            vg = dot(pr, qg_ref[1, e, :, hs], 1, 0).astype(BF)
            for out in home:
                out[:, hs] = vg


def early_kernel(info, v_0, v_1, v_2, c_0, c_1, c_2, out_ref):
    for tile in range(8):
        cols = slice(tile * 256, (tile + 1) * 256)
        acc = jnp.zeros((256, BLOCK), F32)
        for vg, c in ((v_0, c_0), (v_1, c_1), (v_2, c_2)):
            acc = acc + dot(c[:, cols], vg[...], 0, 0)
        for k in range(2):
            out_ref[k, tile * 128 : (tile + 1) * 128, :] = acc[k * 128 : (k + 1) * 128]


def late_rows(half, tile, acc_ref, vg, c):
    cols = [pl.ds(pl.multiple_of((tile * 4 + j * 2 + half) * 128, 128), 128) for j in range(2)]
    left = jnp.concatenate([c[:, at] for at in cols], axis=1)
    return acc_ref[tile * 256 : (tile + 1) * 256, :] + dot(left, vg[...], 0, 0)


def send_kernel(info, acc_ref, vg, c, out_ref):
    for tile in range(4):
        rows = late_rows(1 - info.k, tile, acc_ref, vg, c)
        out_ref[tile * 256 : (tile + 1) * 256, :] = rows.astype(BF)


def keep_kernel(info, acc_ref, vg, c, got_ref, out_ref):
    for tile in range(4):
        acc = late_rows(info.k, tile, acc_ref, vg, c)
        acc = acc + got_ref[tile * 256 : (tile + 1) * 256, :].astype(F32)
        for part in range(4):
            r = tile * 256 + part * 64
            yh, xx, yl = r // 512, (r // 128) % 4, (r // 64) % 2
            out_ref[yh * 2 + yl, xx] = acc[part * 64 : (part + 1) * 64].astype(BF)


def sum_kernel(info, got_ref, out_ref):
    total = jnp.zeros((4, 8, 8, BLOCK), F32)
    for n in range(4):
        total = total + got_ref[n].astype(F32).reshape(4, 8, 8, BLOCK)
    for z in range(8):
        out_ref[z] = total[:, z].reshape(32, BLOCK).astype(BF)


def prods_kernel(
    info, qg_ref, w_oo, w_ot, w_ob, w_po, w_pt, w_pb, p_ref, fac_ref, c0, c1, c2, c3, prod_ref, cross_ref, v_buf
):
    cross = [jnp.zeros((4, QC), F32) for _ in range(2)]
    own = pl.multiple_of(info.yl * 1024, 1024)
    oth = pl.multiple_of((1 - info.yl) * 1024, 1024)
    for n, c in enumerate((c0, c1, c2, c3)):
        _, in_one = source(info, n)
        e = in_one.astype(jnp.int32)
        c_own, c_oth = c[:, pl.ds(own, 1024)], c[:, pl.ds(oth, 1024)]
        for half, (wo, wt, wb) in ((info.k, (w_oo, w_ot, w_ob)), (1 - info.k, (w_po, w_pt, w_pb))):
            v = dot(c_own, wo[...], 1, 0) + dot(c_oth[:, :512], wt[...], 1, 0) + dot(c_oth[:, 512:], wb[...], 1, 0)
            v_buf[:, pl.ds(pl.multiple_of(half * 256, 256), 256)] = v.astype(BF)
        rows = []
        for hh in range(4):
            hs = slice(hh * HD, (hh + 1) * HD)
            prod = dot(v_buf[:, hs], qg_ref[1, e, :, hs], 1, 1)
            prod_ref[n, :, hs] = prod
            pr = p_ref[n, :, hs] * fac_ref[n, hh : hh + 1, :]
            rows.append(jnp.sum(pr * prod, axis=0, keepdims=True))
        part = jnp.concatenate(rows, axis=0)
        cross[0] = cross[0] + jnp.where(in_one, 0.0, part)
        cross[1] = cross[1] + jnp.where(in_one, part, 0.0)
    for e in range(2):
        cross_ref[e] = cross[e]


def grads_kernel(
    info, qg_ref, p_ref, fac_ref, prod_ref, x0, x1, x2, x3, own,
    g0, g1, g2, g3, q0, q1, q2, q3, qp_buf,
):
    qp_buf[...] = jnp.zeros(qp_buf.shape, F32)
    deltas = [x0[e] + x1[e] + x2[e] + x3[e] for e in range(2)]
    for n, out in enumerate((g0, g1, g2, g3)):
        sx, in_one = source(info, n)
        e = in_one.astype(jnp.int32)
        delta = jnp.where(in_one, deltas[1], deltas[0])
        for hh in range(4):
            hs = slice(hh * HD, (hh + 1) * HD)
            pr = p_ref[n, :, hs] * fac_ref[n, hh : hh + 1, :]
            ds = (pr * (prod_ref[n, :, hs] - delta[hh : hh + 1, :])).astype(BF)
            out[:, hs] = (SCALE * dot(ds, qg_ref[0, e, :, hs], 1, 0)).astype(BF)
            qp_buf[e, :, hs] += dot(ds, own[sx, 0:256, hs], 0, 0)
    for out, e, k in (
        (q0, info.yh, info.k), (q1, info.yh, 1 - info.k), (q2, 1 - info.yh, info.k), (q3, 1 - info.yh, 1 - info.k),
    ):
        for x in range(4):
            rows = pl.ds(pl.multiple_of((x * 2 + k) * 16, 16), 16)
            out[x] = (SCALE * qp_buf[e, rows, :]).astype(BF)


def home_kernel(info, b0, b1, b2, b3, out_ref):
    for step, b in enumerate((b0, b1, b2, b3)):
        at = lax.rem(info.x + step, 4) * BLOCK
        out_ref[:, pl.ds(pl.multiple_of(at, BLOCK), BLOCK)] = b[...]


def context_kernel(info, b0, b1, b2, b3, w_oo, w_ot, w_ob, w_po, w_pt, w_pb, out_ref, own_buf, oth_buf):
    for step, b in enumerate((b0, b1, b2, b3)):
        at = pl.ds(pl.multiple_of(lax.rem(info.x + step, 4) * 256, 256), 256)
        own_buf[:, at] = b[:, pl.ds(pl.multiple_of(info.k * 256, 256), 256)]
        oth_buf[:, at] = b[:, pl.ds(pl.multiple_of((1 - info.k) * 256, 256), 256)]
    for base, parts in (
        (info.yl * 1024, ((w_oo, 0, w_po, 0), (w_oo, 512, w_po, 512))),
        ((1 - info.yl) * 1024, ((w_ot, 0, w_pt, 0), (w_ob, 0, w_pb, 0))),
    ):
        for t, (wo, lo, wp, lp) in enumerate(parts):
            acc = dot(own_buf[...], wo[lo : lo + 512, :], 1, 1) + dot(oth_buf[...], wp[lp : lp + 512, :], 1, 1)
            out_ref[:, pl.ds(pl.multiple_of(base + t * 512, 512), 512)] = acc.astype(BF)


def sum_z_kernel(info, got_ref, q0, q1, q2, q3, out_ref):
    total = jnp.zeros((32, BLOCK), F32)
    for n in range(8):
        total = total + got_ref[n].astype(F32)
    out_ref[:, 0:8, :] = total.reshape(4, 8, BLOCK)
    rows = jnp.zeros((4, 16, BLOCK), F32)
    for q in (q0, q1, q2, q3):
        rows = rows + q[...].astype(F32)
    out_ref[:, 8:24, :] = rows


def partners(a):
    core = shift(a, "k", 1)
    return core, shift(a, "yh", 1), shift(core, "yh", 1)


def go_home(parts):
    m1, p1, p2 = parts
    return shift(m1, "x", -1), shift(p2, "x", 2), shift(p1, "x", 1)


def on_device(queries, grad_out, keys, context, value_weight, plan, lengths, blocks):
    yh, xi, ki, yl, zi = (lax.axis_index(a) for a in AXES)
    keys, context = keys[0], context[0]
    run = functools.partial(call, (plan, lengths, blocks))

    pay, w_own = run(
        pack_kernel, "pack", [((4, 304, BLOCK), BF), ((128, 1024), BF)],
        [keys, queries[0], grad_out[0], value_weight], 1, 3, megabytes=60,
    )
    w_oo = lax.all_gather(w_own, "z", axis=0, tiled=True)
    pay = lax.all_to_all(pay, "x", 0, 0)
    (rows,) = run(
        unpack_kernel, "unpack", [((4, 32, BLOCK), BF)], [pay], 1, 1,
        picks={0: (lambda info, r: r.at[:, pl.ds(256, 32)], (4, 32, BLOCK))},
    )
    pay_oth = partners(rows)

    unit = (4, TOK, BLOCK)
    c_m1, c_p1, c_2 = shift(context, "x", 1), shift(context, "x", -1), shift(context, "x", 2)
    c_src = [context, c_m1, c_p1, c_2]

    p, tops, ex, qg = run(
        scores_kernel, "scores",
        [(unit, F32), ((4, 4, QC), F32), ((2, 2, 4, QC), F32), ((2, 2, QC, BLOCK), BF)],
        [pay, *pay_oth], 134, 4,
    )
    v_0, v_m1, v_p1, v_2, u_m1, u_p1, u_2, fac, c_m1, c_p1, w_oo = run(
        probs_kernel, "probs", [((TOK, BLOCK), BF)] * 7 + [((4, 4, QC), F32)],
        [qg, p, tops, ex, *partners(ex)], 134, 4, ties=[c_m1, c_p1, w_oo],
    )
    w_ot = shift(w_oo[:512], ("yh", "yl"), 1)
    w_ob = shift(w_oo[512:], ("yh", "yl"), -1)
    w_all = [w_oo, w_ot, w_ob] + [shift(w, "k", 1) for w in (w_oo, w_ot, w_ob)]
    c_src = [context, c_m1, c_p1, c_2]
    (acc,) = run(
        early_kernel, "block_early", [((2, 1024, BLOCK), F32)], [v_0, v_m1, v_p1] + c_src[:3], 1600, 8,
    )
    picks = {0: (lambda info, r: r.at[1 - info.k], (1024, BLOCK))}
    late = [acc, v_2, c_2]
    (send,) = run(send_kernel, "block_send", [((1024, BLOCK), BF)], late, 270, 4, picks=picks)
    picks = {0: (lambda info, r: r.at[info.k], (1024, BLOCK))}
    pieces, h_m1, h_p1, h_2 = run(
        keep_kernel, "block_keep", [((4, 4, 64, BLOCK), BF)], late + [shift(send, "k", 1)], 270, 5,
        picks=picks, ties=[u_m1, u_p1, u_2],
    )

    got = lax.all_to_all(pieces, ("yh", "yl"), 0, 0)
    prods, cross = run(
        prods_kernel, "prods", [(unit, F32), ((2, 4, QC), F32)],
        [qg, *w_all, p, fac] + c_src, 2300, 10, [((TOK, BLOCK), BF)],
        picks={
            i: (lambda info, r: r.at[:, pl.ds(pl.multiple_of(info.x * 256, 256), 256)], (rows, 256))
            for i, rows in ((1, 1024), (2, 512), (3, 512), (4, 1024), (5, 512), (6, 512))
        },
    )
    g_0, g_m1, g_p1, g_2, q_0, q_k, q_y, q_ky = run(
        grads_kernel, "grads", [((TOK, BLOCK), BF)] * 4 + [((4, 16, BLOCK), BF)] * 4,
        [qg, p, fac, prods, cross, *partners(cross), pay], 270, 6, [((2, QC, BLOCK), F32)],
    )
    z_in, g_m1, g_p1, g_2, q_0 = run(
        sum_kernel, "sum_y", [((8, 32, BLOCK), BF)], [got], 1, 2, ties=[g_m1, g_p1, g_2, q_0],
    )
    both = [(y * 2 + k, (1 - y) * 2 + 1 - k) for y in range(2) for k in range(2)]
    q_rows = [q_0, shift(q_k, "k", 1), shift(q_y, "yh", 1), lax.ppermute(q_ky, ("yh", "k"), both)]
    z_out = lax.all_to_all(z_in, "z", 0, 0)
    (x_in,) = run(sum_z_kernel, "sum_z", [((4, 24, BLOCK), F32)], [z_out, *q_rows], 1, 1)
    x_out = lax.all_to_all(x_in, "x", 0, 0).transpose(1, 0, 2).reshape(24, WIDTH)
    weight_grad, query_grad = x_out[:8], x_out[8:].astype(BF)

    (key_grad,) = run(
        home_kernel, "key_home", [((TOK, WIDTH), BF)], [g_0, *go_home((g_m1, g_p1, g_2))], 1, 2,
    )
    (context_grad,) = run(
        context_kernel, "context_grad", [((TOK, WIDTH), BF)],
        [v_0, *go_home((h_m1, h_p1, h_2)), *w_all], 2200, 10,
        [((TOK, 1024), BF)] * 2,
    )
    return (query_grad[None], key_grad[None], context_grad[None], weight_grad)


def solution(mesh):
    fine = Mesh(mesh.devices.reshape(2, 4, 2, 2, 8), AXES)
    fsdp = ("yl", "z")
    rows = P(fsdp, CTX, None)
    return jax.shard_map(
        on_device,
        mesh=fine,
        in_specs=(rows, rows, rows, rows, P(fsdp, None), P(fsdp, None, None), P(fsdp, None), P(fsdp, CTX)),
        out_specs=(rows, rows, rows, P(AXES, None)),
        check_vma=False,
    )
```

```python
import functools
import math

import jax
import jax.numpy as jnp
from jax import lax
from jax.experimental import pallas as pl
from jax.experimental.pallas import tpu as pltpu
from jax.sharding import Mesh, PartitionSpec as P

HD = 128
QC = 128
HEADS = 16
BLK = 64
TOK = 256
WIDTH = 2048
SCALE = 1.0 / math.sqrt(HD)
NEG = -1e30
BF = jnp.bfloat16
F32 = jnp.float32
CTX = ("yh", "x", "k")
AXES = ("yh", "x", "k", "yl", "z")
VMEM = pl.BlockSpec(memory_space=pltpu.VMEM)
SMEM = pl.BlockSpec(memory_space=pltpu.SMEM)

BLOCK = 256


def params(megabytes):
    return pltpu.CompilerParams(vmem_limit_bytes=megabytes << 20)


def cost(flops, size):
    return pl.CostEstimate(flops=flops, bytes_accessed=size, transcendentals=0)


def dot(a, b, ca, cb):
    return lax.dot_general(a, b, (((ca,), (cb,)), ((), ())), preferred_element_type=F32)


def shift(a, axis, by):
    n = lax.axis_size(axis)
    return lax.ppermute(a, axis, [(i, (i + by) % n) for i in range(n)])


class Info:
    def __init__(self, plan, lengths, blocks):
        self.x, self.k, self.yh, self.yl = (lax.axis_index(a) for a in ("x", "k", "yh", "yl"))
        self.start, self.width = plan[0, 0, 1], plan[0, 1, 1]
        self.lengths = [lengths[0, e] for e in range(2)]
        self.blocks = blocks


class Fetched:
    def __init__(self, src, dst, sem):
        self.copy = pltpu.make_async_copy(src, dst, sem)
        self.ref = dst
        self.copy.start()
        self.pending = True

    def __getitem__(self, at):
        self.ready()
        return self.ref[at]

    def ready(self):
        if self.pending:
            self.copy.wait()
            self.pending = False


def call(scalars, kernel, name, outs, args, flops, size, scratch=(), ties=(), picks=None, megabytes=48):
    n_in, n_out, n_tie = len(args), len(outs), len(ties)
    picks = picks or {}

    def body(plan, lengths, blocks, *refs):
        info = Info(plan, lengths, blocks)
        srcs, refs = refs[:n_in], refs[n_in + n_tie :]
        out_refs, refs = refs[:n_out], refs[n_out + n_tie :]
        bufs, sems, rest = refs[:n_in], refs[n_in], refs[n_in + 1 :]
        srcs = [picks[i][0](info, a) if i in picks else a for i, a in enumerate(srcs)]
        ins = [Fetched(a, b, sems.at[i]) for i, (a, b) in enumerate(zip(srcs, bufs))]
        kernel(info, *ins, *out_refs, *rest)
        for a in ins:
            a.ready()

    anywhere = pl.BlockSpec(memory_space=pl.ANY)
    return pl.pallas_call(
        body,
        in_specs=[SMEM] * 3 + [anywhere] * (n_in + n_tie),
        out_specs=[VMEM] * n_out + [anywhere] * n_tie,
        out_shape=[jax.ShapeDtypeStruct(shape, kind) for shape, kind in outs]
        + [jax.ShapeDtypeStruct(a.shape, a.dtype) for a in ties],
        scratch_shapes=[
            pltpu.VMEM(picks[i][1] if i in picks else a.shape, a.dtype) for i, a in enumerate(args)
        ]
        + [pltpu.SemaphoreType.DMA((n_in,))]
        + [pltpu.VMEM(shape, kind) for shape, kind in scratch],
        input_output_aliases={3 + n_in + i: n_out + i for i in range(n_tie)},
        compiler_params=params(megabytes),
        cost_estimate=cost(1, 1),
        name=name,
    )(*scalars, *args, *ties)


def in_one(info, n):
    c = info.yh * 8 + n
    return (c >= info.start) & (c < info.start + info.width)


def pack_kernel(info, k_ref, q_ref, g_ref, w_ref, out_ref, w_out):
    for b in range(4):
        at = pl.ds(pl.multiple_of(b * 512 + info.k * 256, 256), 256)
        w_out[:, b * 256 : (b + 1) * 256] = w_ref[:, at]
    row = lax.broadcasted_iota(jnp.int32, (16, BLOCK), 0)
    held = jnp.zeros((16, BLOCK), F32)
    for slot in range(TOK // BLK):
        held = jnp.where(row == slot, info.blocks[0, slot].astype(F32), held)
    for j in range(8):
        cols = slice(j * BLOCK, (j + 1) * BLOCK)
        out_ref[j, 256:272, :] = q_ref[:, cols]
        out_ref[j, 272:288, :] = g_ref[:, cols]
        out_ref[j, 288:304, :] = held.astype(BF)
        out_ref[j, 0:256, :] = k_ref[:, cols]


def unpack_kernel(info, pay, out_ref):
    out_ref[...] = pay[...]


def scores_kernel(info, own, far, p_ref, top_ref, ex_ref, qg_ref):
    for which in range(2):
        for i in range(8):
            rows = slice(i * 16, (i + 1) * 16)
            qg_ref[which, info.yh, rows, :] = own[i, 256 + which * 16 : 272 + which * 16, :]
            qg_ref[which, 1 - info.yh, rows, :] = far[i, which * 16 : (which + 1) * 16, :]
    row = lax.broadcasted_iota(jnp.int32, (BLK, QC), 0).astype(F32)
    col = lax.broadcasted_iota(jnp.int32, (BLK, QC), 1).astype(F32)
    tops, sums, ones = [], [], []
    for n in range(8):
        one = in_one(info, n)
        e = one.astype(jnp.int32)
        length = jnp.where(one, info.lengths[1], info.lengths[0]).astype(F32)
        held = own[n, 288:304, 0:QC].astype(F32)
        masks = []
        for slot in range(TOK // BLK):
            b = held[slot : slot + 1, :]
            masks.append((b >= 0.0) & (b * BLK + row <= length - QC + col))
        visible = jnp.concatenate(masks, axis=0)
        top_rows, sum_rows = [], []
        for hh in range(2):
            hs = slice(hh * HD, (hh + 1) * HD)
            masked = jnp.where(visible, dot(own[n, 0:256, hs], qg_ref[0, e, :, hs], 1, 1) * SCALE, NEG)
            top = jnp.max(masked, axis=0, keepdims=True)
            p = jnp.where(visible, jnp.exp(masked - top), 0.0)
            p_ref[n, :, hs] = p
            top_rows.append(top)
            sum_rows.append(jnp.sum(p, axis=0, keepdims=True))
        tops.append(jnp.concatenate(top_rows, axis=0))
        sums.append(jnp.concatenate(sum_rows, axis=0))
        ones.append(one)
        top_ref[n] = tops[n]
    for e in range(2):
        of_e = [one if e else jnp.logical_not(one) for one in ones]
        top = jnp.full((2, QC), NEG, F32)
        for n in range(8):
            top = jnp.maximum(top, jnp.where(of_e[n], tops[n], NEG))
        total = jnp.zeros((2, QC), F32)
        for n in range(8):
            total = total + jnp.where(of_e[n], sums[n] * jnp.exp(tops[n] - top), 0.0)
        ex_ref[0, e] = top
        ex_ref[1, e] = total


def probs_kernel(info, qg_ref, p_ref, top_ref, x0, x1, vg_ref, fac_ref):
    tops, invs = [], []
    for e in range(2):
        top = jnp.maximum(x0[0, e], x1[0, e])
        total = x0[1, e] * jnp.exp(x0[0, e] - top) + x1[1, e] * jnp.exp(x1[0, e] - top)
        tops.append(top)
        invs.append(1.0 / total)
    for n in range(8):
        one = in_one(info, n)
        e = one.astype(jnp.int32)
        factor = jnp.exp(top_ref[n] - jnp.where(one, tops[1], tops[0])) * jnp.where(one, invs[1], invs[0])
        fac_ref[n] = factor
        for hh in range(2):
            hs = slice(hh * HD, (hh + 1) * HD)
            pr = (p_ref[n, :, hs] * factor[hh : hh + 1, :]).astype(BF)
            vg_ref[n, :, hs] = dot(pr, qg_ref[1, e, :, hs], 1, 0).astype(BF)


def ring_index(info, step, other):
    return lax.rem(info.x + step, 4) * 2 + (1 - info.k if other else info.k)


def early_kernel(info, vg, a0, a1, a2, b0, b1, b2, out_ref):
    for tile in range(8):
        cols = slice(tile * 256, (tile + 1) * 256)
        acc = jnp.zeros((256, BLOCK), F32)
        for other, refs in enumerate(((a0, a1, a2), (b0, b1, b2))):
            for step, c in zip((0, 3, 1), refs):
                acc = acc + dot(c[:, cols], vg[ring_index(info, step, other)], 0, 0)
        out_ref[cols, :] = acc


def late_kernel(info, acc_ref, vg, a_top, a_bot, b_top, b_bot, out_ref):
    for tile in range(8):
        cols = slice(tile * 256, (tile + 1) * 256)
        acc = acc_ref[cols, :]
        for other, (top, bot) in enumerate(((a_top, a_bot), (b_top, b_bot))):
            left = jnp.concatenate([top[:, cols], bot[:, cols]], axis=0)
            acc = acc + dot(left, vg[ring_index(info, 2, other)], 0, 0)
        for part in range(4):
            k, yl = part // 2, part % 2
            rows = acc[part * 64 : (part + 1) * 64].astype(BF)
            out_ref[(tile // 4) * 2 + yl, (tile % 4) * 2 + k] = rows


def sum_y_kernel(info, got_ref, out_ref):
    total = jnp.zeros((8, 8, 8, BLOCK), F32)
    for n in range(4):
        total = total + got_ref[n].astype(F32).reshape(8, 8, 8, BLOCK)
    for z in range(8):
        out_ref[z] = total[:, z].reshape(64, BLOCK).astype(BF)


def prods_kernel(info, w_ref, a0, b0, a1, b1, a2, b2, a3, a4, b3, b4, qg_ref, p_ref, fac_ref,
                 prod_ref, cross_ref):
    cross = [jnp.zeros((2, QC), F32) for _ in range(2)]
    turns = (
        (0, 0, (a0,)), (0, 1, (b0,)), (3, 0, (a1,)), (3, 1, (b1,)),
        (1, 0, (a2,)), (1, 1, (b2,)), (2, 0, (a3, a4)), (2, 1, (b3, b4)),
    )
    for step, other, cs in turns:
        n = ring_index(info, step, other)
        one = in_one(info, n)
        e = one.astype(jnp.int32)
        c = jnp.concatenate([c[...] for c in cs], axis=0)
        v = dot(c, w_ref[...], 1, 0).astype(BF)
        rows = []
        for hh in range(2):
            hs = slice(hh * HD, (hh + 1) * HD)
            prod = dot(v[:, hs], qg_ref[1, e, :, hs], 1, 1)
            prod_ref[n, :, hs] = prod
            pr = p_ref[n, :, hs] * fac_ref[n, hh : hh + 1, :]
            rows.append(jnp.sum(pr * prod, axis=0, keepdims=True))
        part = jnp.concatenate(rows, axis=0)
        cross[0] = cross[0] + jnp.where(one, 0.0, part)
        cross[1] = cross[1] + jnp.where(one, part, 0.0)
    for e in range(2):
        cross_ref[e] = cross[e]


def grads_kernel(info, qg_ref, p_ref, fac_ref, prod_ref, x0, x1, own, kg_ref, q_own, q_far, qp_buf):
    qp_buf[...] = jnp.zeros(qp_buf.shape, F32)
    deltas = [x0[e] + x1[e] for e in range(2)]
    for n in range(8):
        one = in_one(info, n)
        e = one.astype(jnp.int32)
        delta = jnp.where(one, deltas[1], deltas[0])
        for hh in range(2):
            hs = slice(hh * HD, (hh + 1) * HD)
            pr = p_ref[n, :, hs] * fac_ref[n, hh : hh + 1, :]
            ds = (pr * (prod_ref[n, :, hs] - delta[hh : hh + 1, :])).astype(BF)
            kg_ref[n, 32:288, hs] = (SCALE * dot(ds, qg_ref[0, e, :, hs], 1, 0)).astype(BF)
            qp_buf[e, :, hs] += dot(ds, own[n, 0:256, hs], 0, 0)
    for out, e in ((q_own, info.yh), (q_far, 1 - info.yh)):
        out[...] = (SCALE * qp_buf[e]).astype(BF).reshape(8, 16, BLOCK)


def join_kernel(got_ref, q0_ref, q1_ref, keys_ref, out_ref, got, q0, q1, rows_ref, sems):
    got, q0, q1 = (
        Fetched(a, b, sems.at[i]) for i, (a, b) in enumerate(((got_ref, got), (q0_ref, q0), (q1_ref, q1)))
    )
    total = jnp.zeros((64, BLOCK), F32)
    for n in range(8):
        total = total + got[n].astype(F32)
    for j in range(8):
        rows = total[j * 8 : (j + 1) * 8]
        high = rows.astype(BF)
        low = rows - high.astype(F32)
        rows_ref[j, 0:16, :] = jnp.concatenate([high.astype(F32), low], axis=0).astype(BF)
        rows_ref[j, 16:32, :] = (q0[j].astype(F32) + q1[j].astype(F32)).astype(BF)
    copy = pltpu.make_async_copy(rows_ref, out_ref.at[:, pl.ds(0, 32)], sems.at[3])
    copy.start()
    copy.wait()


def finish_kernel(info, got_ref, after, w_ref, q_ref, k_ref):
    for j in range(8):
        cols = slice(j * BLOCK, (j + 1) * BLOCK)
        rows = got_ref[j, 0:16, :].astype(F32)
        w_ref[:, cols] = rows[0:8] + rows[8:16]
        q_ref[:, cols] = got_ref[j, 16:32, :]
        k_ref[:, cols] = got_ref[j, 32:288, :]


def context_kernel(info, home, w_own, w_oth, out_ref):
    left = [
        jnp.concatenate([home[b * 2 + k] for b in range(4)], axis=1) for k in (info.k, 1 - info.k)
    ]
    for t in range(4):
        rows = slice(t * 512, (t + 1) * 512)
        out_ref[:, rows] = (dot(left[0], w_own[rows, :], 1, 1) + dot(left[1], w_oth[rows, :], 1, 1)).astype(BF)


def halves_kernel(info, after, m1, p1, m1_out, p1_out):
    m1_out[...] = m1[...]
    p1_out[...] = p1[...]


def on_device(queries, grad_out, keys, context, value_weight, plan, lengths, blocks):
    keys, context = keys[0], context[0]
    run = functools.partial(call, (plan, lengths, blocks))
    ring = ("x", "k")

    pay, w_own = run(
        pack_kernel, "pack", [((8, 304, BLOCK), BF), ((128, 1024), BF)],
        [keys, queries[0], grad_out[0], value_weight], 1, 3, megabytes=60,
    )
    w_own = lax.all_gather(w_own, ("yl", "z"), axis=0, tiled=True)
    pay = lax.all_to_all(pay, ring, 0, 0)
    (rows,) = run(
        unpack_kernel, "unpack", [((8, 32, BLOCK), BF)], [pay], 1, 1,
        picks={0: (lambda info, r: r.at[:, pl.ds(256, 32)], (8, 32, BLOCK))},
    )
    far = shift(rows, "yh", 1)

    c_m1, c_p1 = shift(context, "x", 1), shift(context, "x", -1)

    unit = (8, TOK, BLOCK)
    p, tops, ex, qg = run(
        scores_kernel, "scores",
        [(unit, F32), ((8, 2, QC), F32), ((2, 2, 2, QC), F32), ((2, 2, QC, BLOCK), BF)],
        [pay, far], 134, 4,
    )
    m1_top, p1_bot = run(
        halves_kernel, "halves", [((128, WIDTH), BF)] * 2, [tops, c_m1, c_p1], 1, 3,
        picks={
            1: (lambda info, r: r.at[pl.ds(0, 128)], (128, WIDTH)),
            2: (lambda info, r: r.at[pl.ds(128, 128)], (128, WIDTH)),
        },
    )
    c_own = [context, c_m1, c_p1, shift(m1_top, "x", 1), shift(p1_bot, "x", -1)]
    c_oth = [shift(c, "k", 1) for c in c_own]

    vg, fac = run(
        probs_kernel, "probs", [(unit, BF), ((8, 2, QC), F32)],
        [qg, p, tops, ex, shift(ex, "yh", 1)], 134, 4,
    )
    home = lax.all_to_all(vg, ring, 0, 0)
    (acc,) = run(
        early_kernel, "block_early", [((WIDTH, BLOCK), F32)], [vg] + c_own[:3] + c_oth[:3], 1600, 8,
    )
    pieces, home = run(
        late_kernel, "block_late", [((4, 8, 64, BLOCK), BF)], [acc, vg] + c_own[3:] + c_oth[3:], 540, 4,
        ties=[home],
    )

    got = lax.all_to_all(pieces, ("yh", "yl"), 0, 0)
    pairs = [c for both in zip(c_own[:3], c_oth[:3]) for c in both]
    prods, cross = run(
        prods_kernel, "prods", [(unit, F32), ((2, 2, QC), F32)],
        [w_own] + pairs + c_own[3:] + c_oth[3:] + [qg, p, fac], 2300, 10,
        picks={0: (lambda info, r: r.at[:, pl.ds(pl.multiple_of(info.x * 256, 256), 256)], (WIDTH, BLOCK))},
    )
    z_in, cross, w_own = run(
        sum_y_kernel, "sum_y", [((8, 64, BLOCK), BF)], [got], 1, 2, ties=[cross, w_own], megabytes=60,
    )
    z_out = lax.all_to_all(z_in, "z", 0, 0)
    key_part, q_own, q_far = run(
        grads_kernel, "grads", [((8, 288, BLOCK), BF), ((8, 16, BLOCK), BF), ((8, 16, BLOCK), BF)],
        [qg, p, fac, prods, cross, shift(cross, "yh", 1), pay], 270, 6, [((2, QC, BLOCK), F32)],
    )
    anywhere = pl.BlockSpec(memory_space=pl.ANY)
    rows = (8, 16, BLOCK)
    joined = pl.pallas_call(
        join_kernel,
        in_specs=[anywhere] * 4,
        out_specs=anywhere,
        out_shape=jax.ShapeDtypeStruct((8, 288, BLOCK), BF),
        scratch_shapes=[pltpu.VMEM(shape, BF) for shape in ((8, 64, BLOCK), rows, rows, (8, 32, BLOCK))]
        + [pltpu.SemaphoreType.DMA((4,))],
        input_output_aliases={3: 0},
        compiler_params=params(60),
        cost_estimate=cost(1, 1),
        name="join",
    )(z_out, q_own, shift(q_far, "yh", 1), key_part)
    joined = lax.all_to_all(joined, ring, 0, 0)
    (context_grad,) = run(
        context_kernel, "context_grad", [((TOK, WIDTH), BF)], [home, w_own, shift(w_own, "k", 1)], 2200, 10,
    )
    weight_grad, query_grad, key_grad = run(
        finish_kernel, "finish", [((8, WIDTH), F32), ((16, WIDTH), BF), ((TOK, WIDTH), BF)], [joined, context_grad], 1, 3,
        picks={1: (lambda info, r: r.at[pl.ds(0, 16), pl.ds(0, 128)], (16, 128))},
    )
    return (query_grad[None], key_grad[None], context_grad[None], weight_grad)


def solution(mesh):
    fine = Mesh(mesh.devices.reshape(2, 4, 2, 2, 8), AXES)
    fsdp = ("yl", "z")
    rows = P(fsdp, CTX, None)
    return jax.shard_map(
        on_device,
        mesh=fine,
        in_specs=(rows, rows, rows, rows, P(fsdp, None), P(fsdp, None, None), P(fsdp, None), P(fsdp, CTX)),
        out_specs=(rows, rows, rows, P(AXES, None)),
        check_vma=False,
    )
```

```python
import functools
import math

import jax
import jax.numpy as jnp
from jax import lax
from jax.experimental import pallas as pl
from jax.experimental.pallas import tpu as pltpu
from jax.sharding import Mesh, PartitionSpec as P

HD = 128
QC = 128
HEADS = 16
BLK = 64
TOK = 256
WIDTH = 2048
SCALE = 1.0 / math.sqrt(HD)
NEG = -1e30
BF = jnp.bfloat16
F32 = jnp.float32
CTX = ("yh", "x", "k")
AXES = ("yh", "x", "k", "yl", "z")
VMEM = pl.BlockSpec(memory_space=pltpu.VMEM)
SMEM = pl.BlockSpec(memory_space=pltpu.SMEM)

BLOCK = 256


def params(megabytes):
    return pltpu.CompilerParams(vmem_limit_bytes=megabytes << 20)


def cost(flops, size):
    return pl.CostEstimate(flops=flops, bytes_accessed=size, transcendentals=0)


def dot(a, b, ca, cb):
    return lax.dot_general(a, b, (((ca,), (cb,)), ((), ())), preferred_element_type=F32)


def shift(a, axis, by):
    n = lax.axis_size(axis)
    return lax.ppermute(a, axis, [(i, (i + by) % n) for i in range(n)])


class Info:
    def __init__(self, plan, lengths, blocks):
        self.x, self.k, self.yh, self.yl = (lax.axis_index(a) for a in ("x", "k", "yh", "yl"))
        self.start, self.width = plan[0, 0, 1], plan[0, 1, 1]
        self.lengths = [lengths[0, e] for e in range(2)]
        self.blocks = blocks


class Fetched:
    def __init__(self, src, dst, sem):
        self.copy = pltpu.make_async_copy(src, dst, sem)
        self.ref = dst
        self.copy.start()
        self.pending = True

    def __getitem__(self, at):
        self.ready()
        return self.ref[at]

    def ready(self):
        if self.pending:
            self.copy.wait()
            self.pending = False


def call(scalars, kernel, name, outs, args, flops, size, scratch=(), ties=(), picks=None, stack=(), megabytes=48):
    n_in, n_out, n_tie = len(args), len(outs), len(ties)
    picks = picks or {}
    plain = [i for i in range(n_in) if i not in stack]
    tall = sum(args[i].shape[0] for i in stack)

    def body(plan, lengths, blocks, *refs):
        info = Info(plan, lengths, blocks)
        srcs, refs = refs[:n_in], refs[n_in + n_tie :]
        out_refs, refs = refs[:n_out], refs[n_out + n_tie :]
        bufs, refs = dict(zip(plain, refs)), refs[len(plain) :]
        sems, rest = refs[0], refs[1:]
        at = 0
        for i in stack:
            bufs[i] = rest[0].at[pl.ds(at, args[i].shape[0])]
            at += args[i].shape[0]
        srcs = [picks[i][0](info, a) if i in picks else a for i, a in enumerate(srcs)]
        ins = [Fetched(a, bufs[i], sems.at[i]) for i, a in enumerate(srcs)]
        kernel(info, *ins, *out_refs, *rest)
        for a in ins:
            a.ready()

    anywhere = pl.BlockSpec(memory_space=pl.ANY)
    return pl.pallas_call(
        body,
        in_specs=[SMEM] * 3 + [anywhere] * (n_in + n_tie),
        out_specs=[VMEM] * n_out + [anywhere] * n_tie,
        out_shape=[jax.ShapeDtypeStruct(shape, kind) for shape, kind in outs]
        + [jax.ShapeDtypeStruct(a.shape, a.dtype) for a in ties],
        scratch_shapes=[
            pltpu.VMEM(picks[i][1] if i in picks else args[i].shape, args[i].dtype) for i in plain
        ]
        + [pltpu.SemaphoreType.DMA((n_in,))]
        + ([pltpu.VMEM((tall, args[stack[0]].shape[1]), args[stack[0]].dtype)] if stack else [])
        + [pltpu.VMEM(shape, kind) for shape, kind in scratch],
        input_output_aliases={3 + n_in + i: n_out + i for i in range(n_tie)},
        compiler_params=params(megabytes),
        cost_estimate=cost(1, 1),
        name=name,
    )(*scalars, *args, *ties)


def in_one(info, n):
    c = info.yh * 8 + n
    return (c >= info.start) & (c < info.start + info.width)


def pack_kernel(info, k_ref, q_ref, g_ref, w_ref, out_ref, w_out):
    for b in range(4):
        at = pl.ds(pl.multiple_of(b * 512 + info.k * 256, 256), 256)
        w_out[:, b * 256 : (b + 1) * 256] = w_ref[:, at]
    row = lax.broadcasted_iota(jnp.int32, (16, BLOCK), 0)
    held = jnp.zeros((16, BLOCK), F32)
    for slot in range(TOK // BLK):
        held = jnp.where(row == slot, info.blocks[0, slot].astype(F32), held)
    for j in range(8):
        cols = slice(j * BLOCK, (j + 1) * BLOCK)
        out_ref[j, 256:272, :] = q_ref[:, cols]
        out_ref[j, 272:288, :] = g_ref[:, cols]
        out_ref[j, 288:304, :] = held.astype(BF)
        out_ref[j, 0:256, :] = k_ref[:, cols]


def unpack_kernel(info, pay, out_ref):
    out_ref[...] = pay[...]


def scores_kernel(info, own, far, p_ref, top_ref, ex_ref, qg_ref):
    for which in range(2):
        for i in range(8):
            rows = slice(i * 16, (i + 1) * 16)
            qg_ref[which, info.yh, rows, :] = own[i, 256 + which * 16 : 272 + which * 16, :]
            qg_ref[which, 1 - info.yh, rows, :] = far[i, which * 16 : (which + 1) * 16, :]
    row = lax.broadcasted_iota(jnp.int32, (BLK, QC), 0).astype(F32)
    col = lax.broadcasted_iota(jnp.int32, (BLK, QC), 1).astype(F32)
    tops, sums, ones = [], [], []
    for n in range(8):
        one = in_one(info, n)
        e = one.astype(jnp.int32)
        length = jnp.where(one, info.lengths[1], info.lengths[0]).astype(F32)
        held = own[n, 288:304, 0:QC].astype(F32)
        masks = []
        for slot in range(TOK // BLK):
            b = held[slot : slot + 1, :]
            masks.append((b >= 0.0) & (b * BLK + row <= length - QC + col))
        visible = jnp.concatenate(masks, axis=0)
        top_rows, sum_rows = [], []
        for hh in range(2):
            hs = slice(hh * HD, (hh + 1) * HD)
            masked = jnp.where(visible, dot(own[n, 0:256, hs], qg_ref[0, e, :, hs], 1, 1) * SCALE, NEG)
            top = jnp.max(masked, axis=0, keepdims=True)
            p = jnp.where(visible, jnp.exp(masked - top), 0.0)
            p_ref[n, :, hs] = p
            top_rows.append(top)
            sum_rows.append(jnp.sum(p, axis=0, keepdims=True))
        tops.append(jnp.concatenate(top_rows, axis=0))
        sums.append(jnp.concatenate(sum_rows, axis=0))
        ones.append(one)
        top_ref[n] = tops[n]
    for e in range(2):
        of_e = [one if e else jnp.logical_not(one) for one in ones]
        top = jnp.full((2, QC), NEG, F32)
        for n in range(8):
            top = jnp.maximum(top, jnp.where(of_e[n], tops[n], NEG))
        total = jnp.zeros((2, QC), F32)
        for n in range(8):
            total = total + jnp.where(of_e[n], sums[n] * jnp.exp(tops[n] - top), 0.0)
        ex_ref[0, e] = top
        ex_ref[1, e] = total


def probs_kernel(info, qg_ref, p_ref, top_ref, x0, x1, vg_ref, fac_ref):
    tops, invs = [], []
    for e in range(2):
        top = jnp.maximum(x0[0, e], x1[0, e])
        total = x0[1, e] * jnp.exp(x0[0, e] - top) + x1[1, e] * jnp.exp(x1[0, e] - top)
        tops.append(top)
        invs.append(1.0 / total)
    for n in range(8):
        one = in_one(info, n)
        e = one.astype(jnp.int32)
        factor = jnp.exp(top_ref[n] - jnp.where(one, tops[1], tops[0])) * jnp.where(one, invs[1], invs[0])
        fac_ref[n] = factor
        for hh in range(2):
            hs = slice(hh * HD, (hh + 1) * HD)
            pr = (p_ref[n, :, hs] * factor[hh : hh + 1, :]).astype(BF)
            vg_ref[n, :, hs] = dot(pr, qg_ref[1, e, :, hs], 1, 0).astype(BF)


def ring_index(info, step, other):
    return lax.rem(info.x + step, 4) * 2 + (1 - info.k if other else info.k)


def early_kernel(info, vg, a0, a1, a2, b0, b1, b2, out_ref, mark_ref):
    mark_ref[...] = jnp.zeros(mark_ref.shape, F32)
    for tile in range(8):
        cols = slice(tile * 256, (tile + 1) * 256)
        acc = jnp.zeros((256, BLOCK), F32)
        for other, refs in enumerate(((a0, a1, a2), (b0, b1, b2))):
            for step, c in zip((0, 3, 1), refs):
                acc = acc + dot(c[:, cols], vg[ring_index(info, step, other)], 0, 0)
        out_ref[cols, :] = acc


def late_kernel(info, acc_ref, vg, a_top, a_bot, b_top, b_bot, out_ref):
    for tile in range(8):
        cols = slice(tile * 256, (tile + 1) * 256)
        acc = acc_ref[cols, :]
        for other, (top, bot) in enumerate(((a_top, a_bot), (b_top, b_bot))):
            left = jnp.concatenate([top[:, cols], bot[:, cols]], axis=0)
            acc = acc + dot(left, vg[ring_index(info, 2, other)], 0, 0)
        for part in range(4):
            k, yl = part // 2, part % 2
            rows = acc[part * 64 : (part + 1) * 64].astype(BF)
            out_ref[(tile // 4) * 2 + yl, (tile % 4) * 2 + k] = rows


def sum_y_kernel(info, got_ref, out_ref):
    total = jnp.zeros((8, 8, 8, BLOCK), F32)
    for n in range(4):
        total = total + got_ref[n].astype(F32).reshape(8, 8, 8, BLOCK)
    for z in range(8):
        out_ref[z] = total[:, z].reshape(64, BLOCK).astype(BF)


def prods_kernel(info, w_ref, a0, b0, a1, b1, a2, b2, a3, a4, b3, b4, qg_ref, p_ref, fac_ref,
                 prod_ref, cross_ref, c_buf, v_buf):
    cross = [jnp.zeros((2, QC), F32) for _ in range(2)]
    for c in (a0, b0, a1, b1, a2, b2, a3, a4, b3, b4):
        c.ready()
    v_buf[...] = dot(c_buf[...], w_ref[...], 1, 0).astype(BF)
    turns = (
        (0, 0), (0, 1), (3, 0), (3, 1), (1, 0), (1, 1), (2, 0), (2, 1),
    )
    for at, (step, other) in enumerate(turns):
        n = ring_index(info, step, other)
        one = in_one(info, n)
        e = one.astype(jnp.int32)
        v = v_buf[at * TOK : (at + 1) * TOK, :]
        rows = []
        for hh in range(2):
            hs = slice(hh * HD, (hh + 1) * HD)
            prod = dot(v[:, hs], qg_ref[1, e, :, hs], 1, 1)
            prod_ref[n, :, hs] = prod
            pr = p_ref[n, :, hs] * fac_ref[n, hh : hh + 1, :]
            rows.append(jnp.sum(pr * prod, axis=0, keepdims=True))
        part = jnp.concatenate(rows, axis=0)
        cross[0] = cross[0] + jnp.where(one, 0.0, part)
        cross[1] = cross[1] + jnp.where(one, part, 0.0)
    for e in range(2):
        cross_ref[e] = cross[e]


def grads_kernel(info, qg_ref, p_ref, fac_ref, prod_ref, x0, x1, own, g0, g1, g2, g3, q_own, q_far, qp_buf):
    qp_buf[...] = jnp.zeros(qp_buf.shape, F32)
    deltas = [x0[e] + x1[e] for e in range(2)]
    for step, k in ((step, k) for step in range(4) for k in range(2)):
        n = lax.rem(info.x + step, 4) * 2 + k
        one = in_one(info, n)
        e = one.astype(jnp.int32)
        delta = jnp.where(one, deltas[1], deltas[0])
        for hh in range(2):
            hs = slice(hh * HD, (hh + 1) * HD)
            pr = p_ref[n, :, hs] * fac_ref[n, hh : hh + 1, :]
            ds = (pr * (prod_ref[n, :, hs] - delta[hh : hh + 1, :])).astype(BF)
            (g0, g1, g2, g3)[step][k, :, hs] = (SCALE * dot(ds, qg_ref[0, e, :, hs], 1, 0)).astype(BF)
            qp_buf[e, :, hs] += dot(ds, own[n, 0:256, hs], 0, 0)
    for out, e in ((q_own, info.yh), (q_far, 1 - info.yh)):
        out[...] = (SCALE * qp_buf[e]).astype(BF).reshape(8, 16, BLOCK)


def turn_kernel(info, g0, g1, g2, g3, keep_ref, send_ref):
    for step, g in enumerate((g0, g1, g2, g3)):
        keep_ref[step] = g[info.k]
        send_ref[step] = g[1 - info.k]


def key_kernel(info, keep, got, out_ref):
    for step in range(4):
        for other, part in enumerate((keep, got)):
            at = ring_index(info, 4 - step, other) * BLOCK
            out_ref[:, pl.ds(pl.multiple_of(at, BLOCK), BLOCK)] = part[step]


def join_kernel(info, got_ref, q0, q1, out_ref):
    total = jnp.zeros((64, BLOCK), F32)
    for n in range(8):
        total = total + got_ref[n].astype(F32)
    for j in range(8):
        out_ref[j, 0:8, :] = total[j * 8 : (j + 1) * 8]
        out_ref[j, 8:24, :] = q0[j].astype(F32) + q1[j].astype(F32)


def finish_kernel(info, got_ref, after, after_too, w_ref, q_ref):
    for j in range(8):
        cols = slice(j * BLOCK, (j + 1) * BLOCK)
        w_ref[:, cols] = got_ref[j, 0:8, :]
        q_ref[:, cols] = got_ref[j, 8:24, :].astype(BF)


def after_kernel(info, a, out_ref):
    out_ref[...] = a[...]


def context_kernel(info, home, w_own, w_oth, out_ref):
    left = [
        jnp.concatenate([home[b * 2 + k] for b in range(4)], axis=1) for k in (info.k, 1 - info.k)
    ]
    for t in range(4):
        rows = slice(t * 512, (t + 1) * 512)
        out_ref[:, rows] = (dot(left[0], w_own[rows, :], 1, 1) + dot(left[1], w_oth[rows, :], 1, 1)).astype(BF)


def halves_kernel(after, m1, p1, top_ref, bot_ref, m1_out, p1_out, top, bot, sems):
    copies = [
        pltpu.make_async_copy(m1.at[pl.ds(0, 128)], top, sems.at[0]),
        pltpu.make_async_copy(p1.at[pl.ds(128, 128)], bot, sems.at[1]),
    ]
    for c in copies:
        c.start()
    for c in copies:
        c.wait()
    top_ref[...] = top[...]
    bot_ref[...] = bot[...]


def on_device(queries, grad_out, keys, context, value_weight, plan, lengths, blocks):
    keys, context = keys[0], context[0]
    run = functools.partial(call, (plan, lengths, blocks))
    ring = ("x", "k")

    pay, w_own = run(
        pack_kernel, "pack", [((8, 304, BLOCK), BF), ((128, 1024), BF)],
        [keys, queries[0], grad_out[0], value_weight], 1, 3, megabytes=60,
    )
    w_own = lax.all_gather(w_own, ("yl", "z"), axis=0, tiled=True)
    pay = lax.all_to_all(pay, ring, 0, 0)
    (rows,) = run(
        unpack_kernel, "unpack", [((8, 32, BLOCK), BF)], [pay], 1, 1,
        picks={0: (lambda info, r: r.at[:, pl.ds(256, 32)], (8, 32, BLOCK))},
    )
    far = shift(rows, "yh", 1)

    c_m1, c_p1 = shift(context, "x", 1), shift(context, "x", -1)

    unit = (8, TOK, BLOCK)
    p, tops, ex, qg = run(
        scores_kernel, "scores",
        [(unit, F32), ((8, 2, QC), F32), ((2, 2, 2, QC), F32), ((2, 2, QC, BLOCK), BF)],
        [pay, far], 134, 4,
    )
    ex_far = shift(ex, "yh", 1)
    anywhere = pl.BlockSpec(memory_space=pl.ANY)
    half = jax.ShapeDtypeStruct((128, WIDTH), BF)
    whole = jax.ShapeDtypeStruct((TOK, WIDTH), BF)
    m1_top, p1_bot, c_m1, c_p1 = pl.pallas_call(
        halves_kernel,
        in_specs=[anywhere] * 3,
        out_specs=[VMEM, VMEM, anywhere, anywhere],
        out_shape=[half, half, whole, whole],
        scratch_shapes=[pltpu.VMEM((128, WIDTH), BF)] * 2 + [pltpu.SemaphoreType.DMA((2,))],
        input_output_aliases={1: 2, 2: 3},
        compiler_params=params(60),
        cost_estimate=cost(1, 1),
        name="halves",
    )(ex_far, c_m1, c_p1)
    c_own = [context, c_m1, c_p1, shift(m1_top, "x", 1), shift(p1_bot, "x", -1)]
    c_oth = [shift(c, "k", 1) for c in c_own[:3]]

    vg, fac = run(
        probs_kernel, "probs", [(unit, BF), ((8, 2, QC), F32)],
        [qg, p, tops, ex, ex_far], 134, 4,
    )
    home = lax.all_to_all(vg, ring, 0, 0)
    acc, mark = run(
        early_kernel, "block_early", [((WIDTH, BLOCK), F32), ((8, 128), F32)], [vg] + c_own[:3] + c_oth[:3], 1600, 8,
    )
    _, c_2a, c_2b = run(after_kernel, "after", [((8, 128), F32)], [mark], 1, 1, ties=c_own[3:])
    c_own[3:] = [c_2a, c_2b]
    c_oth = c_oth + [shift(c_2a, "k", 1), shift(c_2b, "k", 1)]
    pieces, home = run(
        late_kernel, "block_late", [((4, 8, 64, BLOCK), BF)], [acc, vg] + c_own[3:] + c_oth[3:], 540, 4,
        ties=[home],
    )

    got = lax.all_to_all(pieces, ("yh", "yl"), 0, 0)
    pairs = [c for both in zip(c_own[:3], c_oth[:3]) for c in both]
    prods, cross = run(
        prods_kernel, "prods", [(unit, F32), ((2, 2, QC), F32)],
        [w_own] + pairs + c_own[3:] + c_oth[3:] + [qg, p, fac], 2300, 10, [((WIDTH, BLOCK), BF)],
        stack=tuple(range(1, 11)),
        picks={0: (lambda info, r: r.at[:, pl.ds(pl.multiple_of(info.x * 256, 256), 256)], (WIDTH, BLOCK))},
    )
    g_0, g_1, g_2, g_3, q_own, q_far = run(
        grads_kernel, "grads", [((2, TOK, BLOCK), BF)] * 4 + [((8, 16, BLOCK), BF)] * 2,
        [qg, p, fac, prods, cross, shift(cross, "yh", 1), pay], 270, 6, [((2, QC, BLOCK), F32)],
    )
    z_in, q_own = run(
        sum_y_kernel, "sum_y", [((8, 64, BLOCK), BF)], [got], 1, 2, ties=[q_own], megabytes=60,
    )
    z_out = lax.all_to_all(z_in, "z", 0, 0)
    g_far = [shift(g_1, "x", 1), shift(g_2, "x", 2), shift(g_3, "x", -1)]
    joined, w_own, *g_far = run(
        join_kernel, "join", [((8, 24, BLOCK), F32)], [z_out, q_own, shift(q_far, "yh", 1)], 1, 1,
        ties=[w_own, *g_far],
    )
    keep, send = run(
        turn_kernel, "turn", [((4, TOK, BLOCK), BF)] * 2,
        [g_0, *g_far], 1, 2,
    )
    (key_grad,) = run(key_kernel, "key_home", [((TOK, WIDTH), BF)], [keep, shift(send, "k", 1)], 1, 2)

    joined = lax.all_to_all(joined, ring, 0, 0)
    (context_grad,) = run(
        context_kernel, "context_grad", [((TOK, WIDTH), BF)], [home, w_own, shift(w_own, "k", 1)], 2200, 10,
    )
    weight_grad, query_grad = run(
        finish_kernel, "finish", [((8, WIDTH), F32), ((16, WIDTH), BF)], [joined, context_grad, key_grad], 1, 1,
        picks={i: (lambda info, r: r.at[pl.ds(0, 16), pl.ds(0, 128)], (16, 128)) for i in (1, 2)},
    )
    return (query_grad[None], key_grad[None], context_grad[None], weight_grad)


def solution(mesh):
    fine = Mesh(mesh.devices.reshape(2, 4, 2, 2, 8), AXES)
    fsdp = ("yl", "z")
    rows = P(fsdp, CTX, None)
    return jax.shard_map(
        on_device,
        mesh=fine,
        in_specs=(rows, rows, rows, rows, P(fsdp, None), P(fsdp, None, None), P(fsdp, None), P(fsdp, CTX)),
        out_specs=(rows, rows, rows, P(AXES, None)),
        check_vma=False,
    )
```

```python
import functools
import math

import jax
import jax.numpy as jnp
from jax import lax
from jax.experimental import pallas as pl
from jax.experimental.pallas import tpu as pltpu
from jax.sharding import Mesh, PartitionSpec as P

HD = 128
QC = 128
HEADS = 16
BLK = 64
TOK = 256
WIDTH = 2048
SCALE = 1.0 / math.sqrt(HD)
NEG = -1e30
BF = jnp.bfloat16
F32 = jnp.float32
CTX = ("yh", "x", "k")
AXES = ("yh", "x", "k", "yl", "z")
VMEM = pl.BlockSpec(memory_space=pltpu.VMEM)
SMEM = pl.BlockSpec(memory_space=pltpu.SMEM)

BLOCK = 256


def params(megabytes):
    return pltpu.CompilerParams(vmem_limit_bytes=megabytes << 20)


def cost(flops, size):
    return pl.CostEstimate(flops=flops, bytes_accessed=size, transcendentals=0)


def dot(a, b, ca, cb):
    return lax.dot_general(a, b, (((ca,), (cb,)), ((), ())), preferred_element_type=F32)


def shift(a, axis, by):
    n = lax.axis_size(axis)
    return lax.ppermute(a, axis, [(i, (i + by) % n) for i in range(n)])


class Info:
    def __init__(self, plan, lengths, blocks):
        self.x, self.k, self.yh, self.yl = (lax.axis_index(a) for a in ("x", "k", "yh", "yl"))
        self.start, self.width = plan[0, 0, 1], plan[0, 1, 1]
        self.lengths = [lengths[0, e] for e in range(2)]
        self.blocks = blocks


class Fetched:
    def __init__(self, src, dst, sem):
        self.copy = pltpu.make_async_copy(src, dst, sem)
        self.ref = dst
        self.copy.start()
        self.pending = True

    def __getitem__(self, at):
        self.ready()
        return self.ref[at]

    def ready(self):
        if self.pending:
            self.copy.wait()
            self.pending = False


def call(scalars, kernel, name, outs, args, flops, size, scratch=(), ties=(), picks=None, stack=(), megabytes=48):
    n_in, n_out, n_tie = len(args), len(outs), len(ties)
    picks = picks or {}
    plain = [i for i in range(n_in) if i not in stack]
    tall = sum(args[i].shape[0] for i in stack)

    def body(plan, lengths, blocks, *refs):
        info = Info(plan, lengths, blocks)
        srcs, refs = refs[:n_in], refs[n_in + n_tie :]
        out_refs, refs = refs[:n_out], refs[n_out + n_tie :]
        bufs, refs = dict(zip(plain, refs)), refs[len(plain) :]
        sems, rest = refs[0], refs[1:]
        at = 0
        for i in stack:
            bufs[i] = rest[0].at[pl.ds(at, args[i].shape[0])]
            at += args[i].shape[0]
        srcs = [picks[i][0](info, a) if i in picks else a for i, a in enumerate(srcs)]
        ins = [Fetched(a, bufs[i], sems.at[i]) for i, a in enumerate(srcs)]
        kernel(info, *ins, *out_refs, *rest)
        for a in ins:
            a.ready()

    anywhere = pl.BlockSpec(memory_space=pl.ANY)
    return pl.pallas_call(
        body,
        in_specs=[SMEM] * 3 + [anywhere] * (n_in + n_tie),
        out_specs=[VMEM] * n_out + [anywhere] * n_tie,
        out_shape=[jax.ShapeDtypeStruct(shape, kind) for shape, kind in outs]
        + [jax.ShapeDtypeStruct(a.shape, a.dtype) for a in ties],
        scratch_shapes=[
            pltpu.VMEM(picks[i][1] if i in picks else args[i].shape, args[i].dtype) for i in plain
        ]
        + [pltpu.SemaphoreType.DMA((n_in,))]
        + ([pltpu.VMEM((tall, args[stack[0]].shape[1]), args[stack[0]].dtype)] if stack else [])
        + [pltpu.VMEM(shape, kind) for shape, kind in scratch],
        input_output_aliases={3 + n_in + i: n_out + i for i in range(n_tie)},
        compiler_params=params(megabytes),
        cost_estimate=cost(1, 1),
        name=name,
    )(*scalars, *args, *ties)


def in_one(info, n):
    c = info.yh * 8 + n
    return (c >= info.start) & (c < info.start + info.width)


def pack_kernel(info, k_ref, q_ref, g_ref, w_ref, out_ref, w_out):
    for b in range(4):
        at = pl.ds(pl.multiple_of(b * 512 + info.k * 256, 256), 256)
        w_out[:, b * 256 : (b + 1) * 256] = w_ref[:, at]
    row = lax.broadcasted_iota(jnp.int32, (16, BLOCK), 0)
    held = jnp.zeros((16, BLOCK), F32)
    for slot in range(TOK // BLK):
        held = jnp.where(row == slot, info.blocks[0, slot].astype(F32), held)
    for j in range(8):
        cols = slice(j * BLOCK, (j + 1) * BLOCK)
        out_ref[j, 256:272, :] = q_ref[:, cols]
        out_ref[j, 272:288, :] = g_ref[:, cols]
        out_ref[j, 288:304, :] = held.astype(BF)
        out_ref[j, 0:256, :] = k_ref[:, cols]


def unpack_kernel(info, pay, out_ref):
    out_ref[...] = pay[...]


def scores_kernel(info, own, far, p_ref, top_ref, ex_ref, qg_ref):
    for which in range(2):
        for i in range(8):
            rows = slice(i * 16, (i + 1) * 16)
            qg_ref[which, info.yh, rows, :] = own[i, 256 + which * 16 : 272 + which * 16, :]
            qg_ref[which, 1 - info.yh, rows, :] = far[i, which * 16 : (which + 1) * 16, :]
    row = lax.broadcasted_iota(jnp.int32, (BLK, QC), 0).astype(F32)
    col = lax.broadcasted_iota(jnp.int32, (BLK, QC), 1).astype(F32)
    tops, sums, ones = [], [], []
    for n in range(8):
        one = in_one(info, n)
        e = one.astype(jnp.int32)
        length = jnp.where(one, info.lengths[1], info.lengths[0]).astype(F32)
        held = own[n, 288:304, 0:QC].astype(F32)
        masks = []
        for slot in range(TOK // BLK):
            b = held[slot : slot + 1, :]
            masks.append((b >= 0.0) & (b * BLK + row <= length - QC + col))
        visible = jnp.concatenate(masks, axis=0)
        top_rows, sum_rows = [], []
        for hh in range(2):
            hs = slice(hh * HD, (hh + 1) * HD)
            masked = jnp.where(visible, dot(own[n, 0:256, hs], qg_ref[0, e, :, hs], 1, 1) * SCALE, NEG)
            top = jnp.max(masked, axis=0, keepdims=True)
            p = jnp.where(visible, jnp.exp(masked - top), 0.0)
            p_ref[n, :, hs] = p
            top_rows.append(top)
            sum_rows.append(jnp.sum(p, axis=0, keepdims=True))
        tops.append(jnp.concatenate(top_rows, axis=0))
        sums.append(jnp.concatenate(sum_rows, axis=0))
        ones.append(one)
        top_ref[n] = tops[n]
    for e in range(2):
        of_e = [one if e else jnp.logical_not(one) for one in ones]
        top = jnp.full((2, QC), NEG, F32)
        for n in range(8):
            top = jnp.maximum(top, jnp.where(of_e[n], tops[n], NEG))
        total = jnp.zeros((2, QC), F32)
        for n in range(8):
            total = total + jnp.where(of_e[n], sums[n] * jnp.exp(tops[n] - top), 0.0)
        ex_ref[0, e] = top
        ex_ref[1, e] = total


def probs_kernel(info, qg_ref, p_ref, top_ref, x0, x1, vg_ref, fac_ref):
    tops, invs = [], []
    for e in range(2):
        top = jnp.maximum(x0[0, e], x1[0, e])
        total = x0[1, e] * jnp.exp(x0[0, e] - top) + x1[1, e] * jnp.exp(x1[0, e] - top)
        tops.append(top)
        invs.append(1.0 / total)
    for n in range(8):
        one = in_one(info, n)
        e = one.astype(jnp.int32)
        factor = jnp.exp(top_ref[n] - jnp.where(one, tops[1], tops[0])) * jnp.where(one, invs[1], invs[0])
        fac_ref[n] = factor
        for hh in range(2):
            hs = slice(hh * HD, (hh + 1) * HD)
            pr = (p_ref[n, :, hs] * factor[hh : hh + 1, :]).astype(BF)
            vg_ref[n, :, hs] = dot(pr, qg_ref[1, e, :, hs], 1, 0).astype(BF)


def ring_index(info, step, other):
    return lax.rem(info.x + step, 4) * 2 + (1 - info.k if other else info.k)


def early_kernel(info, vg, a0, a1, a2, b0, b1, b2, out_ref, mark_ref):
    mark_ref[...] = jnp.zeros(mark_ref.shape, F32)
    for tile in range(8):
        cols = slice(tile * 256, (tile + 1) * 256)
        acc = jnp.zeros((256, BLOCK), F32)
        for other, refs in enumerate(((a0, a1, a2), (b0, b1, b2))):
            for step, c in zip((0, 3, 1), refs):
                acc = acc + dot(c[:, cols], vg[ring_index(info, step, other)], 0, 0)
        out_ref[cols, :] = acc


def late_kernel(info, acc_ref, vg, a_top, a_bot, b_top, b_bot, out_ref):
    for tile in range(8):
        cols = slice(tile * 256, (tile + 1) * 256)
        acc = acc_ref[cols, :]
        for other, (top, bot) in enumerate(((a_top, a_bot), (b_top, b_bot))):
            left = jnp.concatenate([top[:, cols], bot[:, cols]], axis=0)
            acc = acc + dot(left, vg[ring_index(info, 2, other)], 0, 0)
        for part in range(4):
            k, yl = part // 2, part % 2
            rows = acc[part * 64 : (part + 1) * 64].astype(BF)
            out_ref[(tile // 4) * 2 + yl, (tile % 4) * 2 + k] = rows


def sum_y_kernel(info, got_ref, out_ref):
    total = jnp.zeros((8, 8, 8, BLOCK), F32)
    for n in range(4):
        total = total + got_ref[n].astype(F32).reshape(8, 8, 8, BLOCK)
    for z in range(8):
        out_ref[z] = total[:, z].reshape(64, BLOCK).astype(BF)


def prods_kernel(info, w_ref, a0, b0, a1, b1, a2, b2, a3, a4, b3, b4, qg_ref, p_ref, fac_ref,
                 prod_ref, cross_ref, c_buf, v_buf):
    cross = [jnp.zeros((2, QC), F32) for _ in range(2)]
    for c in (a0, b0, a1, b1, a2, b2, a3, a4, b3, b4):
        c.ready()
    v_buf[...] = dot(c_buf[...], w_ref[...], 1, 0).astype(BF)
    turns = (
        (0, 0), (0, 1), (3, 0), (3, 1), (1, 0), (1, 1), (2, 0), (2, 1),
    )
    for at, (step, other) in enumerate(turns):
        n = ring_index(info, step, other)
        one = in_one(info, n)
        e = one.astype(jnp.int32)
        v = v_buf[at * TOK : (at + 1) * TOK, :]
        rows = []
        for hh in range(2):
            hs = slice(hh * HD, (hh + 1) * HD)
            prod = dot(v[:, hs], qg_ref[1, e, :, hs], 1, 1)
            prod_ref[n, :, hs] = prod
            pr = p_ref[n, :, hs] * fac_ref[n, hh : hh + 1, :]
            rows.append(jnp.sum(pr * prod, axis=0, keepdims=True))
        part = jnp.concatenate(rows, axis=0)
        cross[0] = cross[0] + jnp.where(one, 0.0, part)
        cross[1] = cross[1] + jnp.where(one, part, 0.0)
    for e in range(2):
        cross_ref[e] = cross[e]


def grads_kernel(info, qg_ref, p_ref, fac_ref, prod_ref, x0, x1, own, g0, g1, g2, g3, q_own, q_far, qp_buf):
    qp_buf[...] = jnp.zeros(qp_buf.shape, F32)
    deltas = [x0[e] + x1[e] for e in range(2)]
    for step, k in ((step, k) for step in range(4) for k in range(2)):
        n = lax.rem(info.x + step, 4) * 2 + k
        one = in_one(info, n)
        e = one.astype(jnp.int32)
        delta = jnp.where(one, deltas[1], deltas[0])
        for hh in range(2):
            hs = slice(hh * HD, (hh + 1) * HD)
            pr = p_ref[n, :, hs] * fac_ref[n, hh : hh + 1, :]
            ds = (pr * (prod_ref[n, :, hs] - delta[hh : hh + 1, :])).astype(BF)
            (g0, g1, g2, g3)[step][k, :, hs] = (SCALE * dot(ds, qg_ref[0, e, :, hs], 1, 0)).astype(BF)
            qp_buf[e, :, hs] += dot(ds, own[n, 0:256, hs], 0, 0)
    for out, e in ((q_own, info.yh), (q_far, 1 - info.yh)):
        out[...] = (SCALE * qp_buf[e]).astype(BF).reshape(8, 16, BLOCK)


def turn_kernel(info, g0, g1, g2, g3, keep_ref, send_ref):
    for step, g in enumerate((g0, g1, g2, g3)):
        keep_ref[step] = g[info.k]
        send_ref[step] = g[1 - info.k]


def key_kernel(info, keep, got, out_ref):
    for step in range(4):
        for other, part in enumerate((keep, got)):
            at = ring_index(info, 4 - step, other) * BLOCK
            out_ref[:, pl.ds(pl.multiple_of(at, BLOCK), BLOCK)] = part[step]


def join_kernel(info, got_ref, q0, q1, out_ref):
    total = jnp.zeros((64, BLOCK), F32)
    for n in range(8):
        total = total + got_ref[n].astype(F32)
    for j in range(8):
        out_ref[j, 0:8, :] = total[j * 8 : (j + 1) * 8]
        out_ref[j, 8:24, :] = q0[j].astype(F32) + q1[j].astype(F32)


def finish_kernel(info, got_ref, after, after_too, w_ref, q_ref):
    for j in range(8):
        cols = slice(j * BLOCK, (j + 1) * BLOCK)
        w_ref[:, cols] = got_ref[j, 0:8, :]
        q_ref[:, cols] = got_ref[j, 8:24, :].astype(BF)


def after_kernel(info, a, out_ref):
    out_ref[...] = a[...]


def context_kernel(info, home, w_own, w_oth, out_ref):
    left = [
        jnp.concatenate([home[b * 2 + k] for b in range(4)], axis=1) for k in (info.k, 1 - info.k)
    ]
    for t in range(4):
        rows = slice(t * 512, (t + 1) * 512)
        out_ref[:, rows] = (dot(left[0], w_own[rows, :], 1, 1) + dot(left[1], w_oth[rows, :], 1, 1)).astype(BF)


def halves_kernel(after, m1, p1, top_ref, bot_ref, m1_out, p1_out, top, bot, sems):
    copies = [
        pltpu.make_async_copy(m1.at[pl.ds(0, 128)], top, sems.at[0]),
        pltpu.make_async_copy(p1.at[pl.ds(128, 128)], bot, sems.at[1]),
    ]
    for c in copies:
        c.start()
    for c in copies:
        c.wait()
    top_ref[...] = top[...]
    bot_ref[...] = bot[...]


def on_device(queries, grad_out, keys, context, value_weight, plan, lengths, blocks):
    keys, context = keys[0], context[0]
    run = functools.partial(call, (plan, lengths, blocks))
    ring = ("x", "k")

    pay, w_own = run(
        pack_kernel, "pack", [((8, 304, BLOCK), BF), ((128, 1024), BF)],
        [keys, queries[0], grad_out[0], value_weight], 1, 3, megabytes=60,
    )
    w_own = lax.all_gather(w_own, ("yl", "z"), axis=0, tiled=True)
    pay = lax.all_to_all(pay, ring, 0, 0)
    (rows,) = run(
        unpack_kernel, "unpack", [((8, 32, BLOCK), BF)], [pay], 1, 1,
        picks={0: (lambda info, r: r.at[:, pl.ds(256, 32)], (8, 32, BLOCK))},
    )
    far = shift(rows, "yh", 1)

    c_m1, c_p1 = shift(context, "x", 1), shift(context, "x", -1)

    unit = (8, TOK, BLOCK)
    p, tops, ex, qg = run(
        scores_kernel, "scores",
        [(unit, F32), ((8, 2, QC), F32), ((2, 2, 2, QC), F32), ((2, 2, QC, BLOCK), BF)],
        [pay, far], 134, 4,
    )
    ex_far = shift(ex, "yh", 1)
    anywhere = pl.BlockSpec(memory_space=pl.ANY)
    half = jax.ShapeDtypeStruct((128, WIDTH), BF)
    whole = jax.ShapeDtypeStruct((TOK, WIDTH), BF)
    m1_top, p1_bot, c_m1, c_p1 = pl.pallas_call(
        halves_kernel,
        in_specs=[anywhere] * 3,
        out_specs=[VMEM, VMEM, anywhere, anywhere],
        out_shape=[half, half, whole, whole],
        scratch_shapes=[pltpu.VMEM((128, WIDTH), BF)] * 2 + [pltpu.SemaphoreType.DMA((2,))],
        input_output_aliases={1: 2, 2: 3},
        compiler_params=params(60),
        cost_estimate=cost(1, 1),
        name="halves",
    )(ex_far, c_m1, c_p1)
    c_own = [context, c_m1, c_p1, shift(m1_top, "x", 1), shift(p1_bot, "x", -1)]
    c_oth = [shift(c, "k", 1) for c in c_own[:3]]

    vg, fac = run(
        probs_kernel, "probs", [(unit, BF), ((8, 2, QC), F32)],
        [qg, p, tops, ex, ex_far], 134, 4,
    )
    home = lax.all_to_all(vg, ring, 0, 0)
    acc, mark = run(
        early_kernel, "block_early", [((WIDTH, BLOCK), F32), ((8, 128), F32)], [vg] + c_own[:3] + c_oth[:3], 1600, 8,
    )
    _, c_2a, c_2b = run(after_kernel, "after", [((8, 128), F32)], [mark], 1, 1, ties=c_own[3:])
    c_own[3:] = [c_2a, c_2b]
    c_oth = c_oth + [shift(c_2a, "k", 1), shift(c_2b, "k", 1)]
    (pieces,) = run(
        late_kernel, "block_late", [((4, 8, 64, BLOCK), BF)], [acc, vg] + c_own[3:] + c_oth[3:], 540, 4,
    )

    got = lax.all_to_all(pieces, ("yh", "yl"), 0, 0)
    pairs = [c for both in zip(c_own[:3], c_oth[:3]) for c in both]
    prods, cross, home = run(
        prods_kernel, "prods", [(unit, F32), ((2, 2, QC), F32)],
        [w_own] + pairs + c_own[3:] + c_oth[3:] + [qg, p, fac], 2300, 10, [((WIDTH, BLOCK), BF)],
        stack=tuple(range(1, 11)),
        picks={0: (lambda info, r: r.at[:, pl.ds(pl.multiple_of(info.x * 256, 256), 256)], (WIDTH, BLOCK))},
        ties=[home],
    )
    g_0, g_1, g_2, g_3, q_own, q_far = run(
        grads_kernel, "grads", [((2, TOK, BLOCK), BF)] * 4 + [((8, 16, BLOCK), BF)] * 2,
        [qg, p, fac, prods, cross, shift(cross, "yh", 1), pay], 270, 6, [((2, QC, BLOCK), F32)],
    )
    z_in, q_own = run(
        sum_y_kernel, "sum_y", [((8, 64, BLOCK), BF)], [got], 1, 2, ties=[q_own], megabytes=60,
    )
    z_out = lax.all_to_all(z_in, "z", 0, 0)
    g_far = [shift(g_1, "x", 1), shift(g_2, "x", 2), shift(g_3, "x", -1)]
    joined, w_own, *g_far = run(
        join_kernel, "join", [((8, 24, BLOCK), F32)], [z_out, q_own, shift(q_far, "yh", 1)], 1, 1,
        ties=[w_own, *g_far],
    )
    keep, send = run(
        turn_kernel, "turn", [((4, TOK, BLOCK), BF)] * 2,
        [g_0, *g_far], 1, 2,
    )
    (key_grad,) = run(key_kernel, "key_home", [((TOK, WIDTH), BF)], [keep, shift(send, "k", 1)], 1, 2)

    joined = lax.all_to_all(joined, ring, 0, 0)
    (context_grad,) = run(
        context_kernel, "context_grad", [((TOK, WIDTH), BF)], [home, w_own, shift(w_own, "k", 1)], 2200, 10,
    )
    weight_grad, query_grad = run(
        finish_kernel, "finish", [((8, WIDTH), F32), ((16, WIDTH), BF)], [joined, context_grad, key_grad], 1, 1,
        picks={i: (lambda info, r: r.at[pl.ds(0, 16), pl.ds(0, 128)], (16, 128)) for i in (1, 2)},
    )
    return (query_grad[None], key_grad[None], context_grad[None], weight_grad)


def solution(mesh):
    fine = Mesh(mesh.devices.reshape(2, 4, 2, 2, 8), AXES)
    fsdp = ("yl", "z")
    rows = P(fsdp, CTX, None)
    return jax.shard_map(
        on_device,
        mesh=fine,
        in_specs=(rows, rows, rows, rows, P(fsdp, None), P(fsdp, None, None), P(fsdp, None), P(fsdp, CTX)),
        out_specs=(rows, rows, rows, P(AXES, None)),
        check_vma=False,
    )
```

```python
import functools
import math

import jax
import jax.numpy as jnp
from jax import lax
from jax.experimental import pallas as pl
from jax.experimental.pallas import tpu as pltpu
from jax.sharding import Mesh, PartitionSpec as P

HD = 128
QC = 128
HEADS = 16
BLK = 64
TOK = 256
WIDTH = 2048
SCALE = 1.0 / math.sqrt(HD)
NEG = -1e30
BF = jnp.bfloat16
F32 = jnp.float32
CTX = ("yh", "x", "k")
AXES = ("yh", "x", "k", "yl", "z")
VMEM = pl.BlockSpec(memory_space=pltpu.VMEM)
SMEM = pl.BlockSpec(memory_space=pltpu.SMEM)

BLOCK = 256


def params(megabytes):
    return pltpu.CompilerParams(vmem_limit_bytes=megabytes << 20)


def cost(flops, size):
    return pl.CostEstimate(flops=flops, bytes_accessed=size, transcendentals=0)


def dot(a, b, ca, cb):
    return lax.dot_general(a, b, (((ca,), (cb,)), ((), ())), preferred_element_type=F32)


def shift(a, axis, by):
    n = lax.axis_size(axis)
    return lax.ppermute(a, axis, [(i, (i + by) % n) for i in range(n)])


class Info:
    def __init__(self, plan, lengths, blocks):
        self.x, self.k, self.yh, self.yl = (lax.axis_index(a) for a in ("x", "k", "yh", "yl"))
        self.start, self.width = plan[0, 0, 1], plan[0, 1, 1]
        self.lengths = [lengths[0, e] for e in range(2)]
        self.blocks = blocks


class Fetched:
    def __init__(self, src, dst, sem):
        self.copy = pltpu.make_async_copy(src, dst, sem)
        self.ref = dst
        self.copy.start()
        self.pending = True

    def __getitem__(self, at):
        self.ready()
        return self.ref[at]

    def ready(self):
        if self.pending:
            self.copy.wait()
            self.pending = False


def call(scalars, kernel, name, outs, args, flops, size, scratch=(), ties=(), picks=None, stack=(), megabytes=48):
    n_in, n_out, n_tie = len(args), len(outs), len(ties)
    picks = picks or {}
    plain = [i for i in range(n_in) if i not in stack]
    tall = sum(args[i].shape[0] for i in stack)

    def body(plan, lengths, blocks, *refs):
        info = Info(plan, lengths, blocks)
        srcs, refs = refs[:n_in], refs[n_in + n_tie :]
        out_refs, refs = refs[:n_out], refs[n_out + n_tie :]
        bufs, refs = dict(zip(plain, refs)), refs[len(plain) :]
        sems, rest = refs[0], refs[1:]
        at = 0
        for i in stack:
            bufs[i] = rest[0].at[pl.ds(at, args[i].shape[0])]
            at += args[i].shape[0]
        srcs = [picks[i][0](info, a) if i in picks else a for i, a in enumerate(srcs)]
        ins = [Fetched(a, bufs[i], sems.at[i]) for i, a in enumerate(srcs)]
        kernel(info, *ins, *out_refs, *rest)
        for a in ins:
            a.ready()

    anywhere = pl.BlockSpec(memory_space=pl.ANY)
    return pl.pallas_call(
        body,
        in_specs=[SMEM] * 3 + [anywhere] * (n_in + n_tie),
        out_specs=[VMEM] * n_out + [anywhere] * n_tie,
        out_shape=[jax.ShapeDtypeStruct(shape, kind) for shape, kind in outs]
        + [jax.ShapeDtypeStruct(a.shape, a.dtype) for a in ties],
        scratch_shapes=[
            pltpu.VMEM(picks[i][1] if i in picks else args[i].shape, args[i].dtype) for i in plain
        ]
        + [pltpu.SemaphoreType.DMA((n_in,))]
        + ([pltpu.VMEM((tall, args[stack[0]].shape[1]), args[stack[0]].dtype)] if stack else [])
        + [pltpu.VMEM(shape, kind) for shape, kind in scratch],
        input_output_aliases={3 + n_in + i: n_out + i for i in range(n_tie)},
        compiler_params=params(megabytes),
        cost_estimate=cost(1, 1),
        name=name,
    )(*scalars, *args, *ties)


def in_one(info, n):
    c = info.yh * 8 + n
    return (c >= info.start) & (c < info.start + info.width)


def pack_kernel(info, k_ref, q_ref, g_ref, w_ref, out_ref, w_out):
    for b in range(4):
        at = pl.ds(pl.multiple_of(b * 512 + info.k * 256, 256), 256)
        w_out[:, b * 256 : (b + 1) * 256] = w_ref[:, at]
    row = lax.broadcasted_iota(jnp.int32, (16, BLOCK), 0)
    held = jnp.zeros((16, BLOCK), F32)
    for slot in range(TOK // BLK):
        held = jnp.where(row == slot, info.blocks[0, slot].astype(F32), held)
    for j in range(8):
        cols = slice(j * BLOCK, (j + 1) * BLOCK)
        out_ref[j, 256:272, :] = q_ref[:, cols]
        out_ref[j, 272:288, :] = g_ref[:, cols]
        out_ref[j, 288:304, :] = held.astype(BF)
        out_ref[j, 0:256, :] = k_ref[:, cols]


def unpack_kernel(info, pay, out_ref):
    out_ref[...] = pay[...]


def scores_kernel(info, own, far, p_ref, top_ref, ex_ref, qg_ref):
    for which in range(2):
        for i in range(8):
            rows = slice(i * 16, (i + 1) * 16)
            qg_ref[which, info.yh, rows, :] = own[i, 256 + which * 16 : 272 + which * 16, :]
            qg_ref[which, 1 - info.yh, rows, :] = far[i, which * 16 : (which + 1) * 16, :]
    row = lax.broadcasted_iota(jnp.int32, (BLK, QC), 0).astype(F32)
    col = lax.broadcasted_iota(jnp.int32, (BLK, QC), 1).astype(F32)
    tops, sums, ones = [], [], []
    for n in range(8):
        one = in_one(info, n)
        e = one.astype(jnp.int32)
        length = jnp.where(one, info.lengths[1], info.lengths[0]).astype(F32)
        held = own[n, 288:304, 0:QC].astype(F32)
        masks = []
        for slot in range(TOK // BLK):
            b = held[slot : slot + 1, :]
            masks.append((b >= 0.0) & (b * BLK + row <= length - QC + col))
        visible = jnp.concatenate(masks, axis=0)
        top_rows, sum_rows = [], []
        for hh in range(2):
            hs = slice(hh * HD, (hh + 1) * HD)
            masked = jnp.where(visible, dot(own[n, 0:256, hs], qg_ref[0, e, :, hs], 1, 1) * SCALE, NEG)
            top = jnp.max(masked, axis=0, keepdims=True)
            p = jnp.where(visible, jnp.exp(masked - top), 0.0)
            p_ref[n, :, hs] = p.astype(BF)
            top_rows.append(top)
            sum_rows.append(jnp.sum(p, axis=0, keepdims=True))
        tops.append(jnp.concatenate(top_rows, axis=0))
        sums.append(jnp.concatenate(sum_rows, axis=0))
        ones.append(one)
        top_ref[n] = tops[n]
    for e in range(2):
        of_e = [one if e else jnp.logical_not(one) for one in ones]
        top = jnp.full((2, QC), NEG, F32)
        for n in range(8):
            top = jnp.maximum(top, jnp.where(of_e[n], tops[n], NEG))
        total = jnp.zeros((2, QC), F32)
        for n in range(8):
            total = total + jnp.where(of_e[n], sums[n] * jnp.exp(tops[n] - top), 0.0)
        ex_ref[0, e] = top
        ex_ref[1, e] = total


def probs_kernel(info, qg_ref, p_ref, top_ref, x0, x1, vg_ref, u0, u1, u2, u3, fac_ref):
    tops, invs = [], []
    for e in range(2):
        top = jnp.maximum(x0[0, e], x1[0, e])
        total = x0[1, e] * jnp.exp(x0[0, e] - top) + x1[1, e] * jnp.exp(x1[0, e] - top)
        tops.append(top)
        invs.append(1.0 / total)
    for n in range(8):
        one = in_one(info, n)
        e = one.astype(jnp.int32)
        factor = jnp.exp(top_ref[n] - jnp.where(one, tops[1], tops[0])) * jnp.where(one, invs[1], invs[0])
        fac_ref[n] = factor
        for hh in range(2):
            hs = slice(hh * HD, (hh + 1) * HD)
            pr = (p_ref[n, :, hs].astype(F32) * factor[hh : hh + 1, :]).astype(BF)
            vg_ref[n, :, hs] = dot(pr, qg_ref[1, e, :, hs], 1, 0).astype(BF)
    for step, u in enumerate((u0, u1, u2, u3)):
        for k in range(2):
            u[k] = vg_ref[lax.rem(info.x + step, 4) * 2 + k]


def ring_index(info, step, other):
    return lax.rem(info.x + step, 4) * 2 + (1 - info.k if other else info.k)


def early_kernel(info, vg, a0, a1, a2, b0, b1, b2, out_ref, mark_ref):
    mark_ref[...] = jnp.zeros(mark_ref.shape, F32)
    for tile in range(8):
        cols = slice(tile * 256, (tile + 1) * 256)
        acc = jnp.zeros((256, BLOCK), F32)
        for other, refs in enumerate(((a0, a1, a2), (b0, b1, b2))):
            for step, c in zip((0, 3, 1), refs):
                acc = acc + dot(c[:, cols], vg[ring_index(info, step, other)], 0, 0)
        out_ref[cols, :] = acc


def late_kernel(info, acc_ref, vg, a_top, a_bot, b_top, b_bot, out_ref):
    for tile in range(8):
        cols = slice(tile * 256, (tile + 1) * 256)
        acc = acc_ref[cols, :]
        for other, (top, bot) in enumerate(((a_top, a_bot), (b_top, b_bot))):
            left = jnp.concatenate([top[:, cols], bot[:, cols]], axis=0)
            acc = acc + dot(left, vg[ring_index(info, 2, other)], 0, 0)
        for part in range(4):
            k, yl = part // 2, part % 2
            rows = acc[part * 64 : (part + 1) * 64].astype(BF)
            out_ref[(tile // 4) * 2 + yl, (tile % 4) * 2 + k] = rows


def sum_y_kernel(info, got_ref, out_ref):
    total = jnp.zeros((8, 8, 8, BLOCK), F32)
    for n in range(4):
        total = total + got_ref[n].astype(F32).reshape(8, 8, 8, BLOCK)
    for z in range(8):
        out_ref[z] = total[:, z].reshape(64, BLOCK).astype(BF)


def prods_kernel(info, w_ref, a0, b0, a1, b1, a2, b2, a3, a4, b3, b4, qg_ref, p_ref, fac_ref,
                 prod_ref, cross_ref, c_buf, v_buf):
    cross = [jnp.zeros((2, QC), F32) for _ in range(2)]
    for c in (a0, b0, a1, b1, a2, b2, a3, a4, b3, b4):
        c.ready()
    v_buf[...] = dot(c_buf[...], w_ref[...], 1, 0).astype(BF)
    turns = (
        (0, 0), (0, 1), (3, 0), (3, 1), (1, 0), (1, 1), (2, 0), (2, 1),
    )
    for at, (step, other) in enumerate(turns):
        n = ring_index(info, step, other)
        one = in_one(info, n)
        e = one.astype(jnp.int32)
        v = v_buf[at * TOK : (at + 1) * TOK, :]
        rows = []
        for hh in range(2):
            hs = slice(hh * HD, (hh + 1) * HD)
            prod = dot(v[:, hs], qg_ref[1, e, :, hs], 1, 1)
            prod_ref[n, :, hs] = prod
            pr = p_ref[n, :, hs].astype(F32) * fac_ref[n, hh : hh + 1, :]
            rows.append(jnp.sum(pr * prod, axis=0, keepdims=True))
        part = jnp.concatenate(rows, axis=0)
        cross[0] = cross[0] + jnp.where(one, 0.0, part)
        cross[1] = cross[1] + jnp.where(one, part, 0.0)
    for e in range(2):
        cross_ref[e] = cross[e]


def grads_kernel(info, qg_ref, p_ref, fac_ref, prod_ref, x0, x1, own, g0, g1, g2, g3, q_own, q_far, qp_buf):
    qp_buf[...] = jnp.zeros(qp_buf.shape, F32)
    deltas = [x0[e] + x1[e] for e in range(2)]
    for step, k in ((step, k) for step in range(4) for k in range(2)):
        n = lax.rem(info.x + step, 4) * 2 + k
        one = in_one(info, n)
        e = one.astype(jnp.int32)
        delta = jnp.where(one, deltas[1], deltas[0])
        for hh in range(2):
            hs = slice(hh * HD, (hh + 1) * HD)
            pr = p_ref[n, :, hs].astype(F32) * fac_ref[n, hh : hh + 1, :]
            ds = (pr * (prod_ref[n, :, hs] - delta[hh : hh + 1, :])).astype(BF)
            (g0, g1, g2, g3)[step][k, :, hs] = (SCALE * dot(ds, qg_ref[0, e, :, hs], 1, 0)).astype(BF)
            qp_buf[e, :, hs] += dot(ds, own[n, 0:256, hs], 0, 0)
    for out, e in ((q_own, info.yh), (q_far, 1 - info.yh)):
        out[...] = (SCALE * qp_buf[e]).astype(BF).reshape(8, 16, BLOCK)


def turn_kernel(info, g0, g1, g2, g3, u0, u1, u2, u3, keep_ref, send_ref):
    for n, part in enumerate((g0, g1, g2, g3, u0, u1, u2, u3)):
        keep_ref[n] = part[info.k]
        send_ref[n] = part[1 - info.k]


def key_kernel(info, keep, got, out_ref):
    for step in range(4):
        for other, part in enumerate((keep, got)):
            at = ring_index(info, 4 - step, other) * BLOCK
            out_ref[:, pl.ds(pl.multiple_of(at, BLOCK), BLOCK)] = part[step]


def join_kernel(info, got_ref, q0, q1, out_ref):
    total = jnp.zeros((64, BLOCK), F32)
    for n in range(8):
        total = total + got_ref[n].astype(F32)
    for j in range(8):
        out_ref[j, 0:8, :] = total[j * 8 : (j + 1) * 8]
        out_ref[j, 8:24, :] = q0[j].astype(F32) + q1[j].astype(F32)


def finish_kernel(info, got_ref, after, after_too, w_ref, q_ref):
    for j in range(8):
        cols = slice(j * BLOCK, (j + 1) * BLOCK)
        w_ref[:, cols] = got_ref[j, 0:8, :]
        q_ref[:, cols] = got_ref[j, 8:24, :].astype(BF)


def after_kernel(info, a, out_ref):
    out_ref[...] = a[...]


def context_kernel(info, keep, got, w_own, w_oth, out_ref):
    left = [
        jnp.concatenate([part[lax.rem(info.x + 4 - b, 4)] for b in range(4)], axis=1) for part in (keep, got)
    ]
    for t in range(4):
        rows = slice(t * 512, (t + 1) * 512)
        out_ref[:, rows] = (dot(left[0], w_own[rows, :], 1, 1) + dot(left[1], w_oth[rows, :], 1, 1)).astype(BF)


def halves_kernel(after, m1, p1, top_ref, bot_ref, m1_out, p1_out, top, bot, sems):
    copies = [
        pltpu.make_async_copy(m1.at[pl.ds(0, 128)], top, sems.at[0]),
        pltpu.make_async_copy(p1.at[pl.ds(128, 128)], bot, sems.at[1]),
    ]
    for c in copies:
        c.start()
    for c in copies:
        c.wait()
    top_ref[...] = top[...]
    bot_ref[...] = bot[...]


def on_device(queries, grad_out, keys, context, value_weight, plan, lengths, blocks):
    keys, context = keys[0], context[0]
    run = functools.partial(call, (plan, lengths, blocks))
    ring = ("x", "k")

    pay, w_own = run(
        pack_kernel, "pack", [((8, 304, BLOCK), BF), ((128, 1024), BF)],
        [keys, queries[0], grad_out[0], value_weight], 1, 3, megabytes=60,
    )
    w_own = lax.all_gather(w_own, ("yl", "z"), axis=0, tiled=True)
    pay = lax.all_to_all(pay, ring, 0, 0)
    (rows,) = run(
        unpack_kernel, "unpack", [((8, 32, BLOCK), BF)], [pay], 1, 1,
        picks={0: (lambda info, r: r.at[:, pl.ds(256, 32)], (8, 32, BLOCK))},
    )
    far = shift(rows, "yh", 1)

    c_m1, c_p1 = shift(context, "x", 1), shift(context, "x", -1)

    unit = (8, TOK, BLOCK)
    p, tops, ex, qg = run(
        scores_kernel, "scores",
        [(unit, BF), ((8, 2, QC), F32), ((2, 2, 2, QC), F32), ((2, 2, QC, BLOCK), BF)],
        [pay, far], 134, 4,
    )
    ex_far = shift(ex, "yh", 1)
    anywhere = pl.BlockSpec(memory_space=pl.ANY)
    half = jax.ShapeDtypeStruct((128, WIDTH), BF)
    whole = jax.ShapeDtypeStruct((TOK, WIDTH), BF)
    m1_top, p1_bot, c_m1, c_p1 = pl.pallas_call(
        halves_kernel,
        in_specs=[anywhere] * 3,
        out_specs=[VMEM, VMEM, anywhere, anywhere],
        out_shape=[half, half, whole, whole],
        scratch_shapes=[pltpu.VMEM((128, WIDTH), BF)] * 2 + [pltpu.SemaphoreType.DMA((2,))],
        input_output_aliases={1: 2, 2: 3},
        compiler_params=params(60),
        cost_estimate=cost(1, 1),
        name="halves",
    )(ex_far, c_m1, c_p1)
    c_own = [context, c_m1, c_p1, shift(m1_top, "x", 1), shift(p1_bot, "x", -1)]
    c_oth = [shift(c, "k", 1) for c in c_own[:3]]

    vg, u_0, u_1, u_2, u_3, fac = run(
        probs_kernel, "probs", [(unit, BF)] + [((2, TOK, BLOCK), BF)] * 4 + [((8, 2, QC), F32)],
        [qg, p, tops, ex, ex_far], 134, 4,
    )
    acc, mark = run(
        early_kernel, "block_early", [((WIDTH, BLOCK), F32), ((8, 128), F32)], [vg] + c_own[:3] + c_oth[:3], 1600, 8,
    )
    _, c_2a, c_2b = run(after_kernel, "after", [((8, 128), F32)], [mark], 1, 1, ties=c_own[3:])
    c_own[3:] = [c_2a, c_2b]
    c_oth = c_oth + [shift(c_2a, "k", 1), shift(c_2b, "k", 1)]
    pieces, u_1, u_2, u_3 = run(
        late_kernel, "block_late", [((4, 8, 64, BLOCK), BF)], [acc, vg] + c_own[3:] + c_oth[3:], 540, 4,
        ties=[u_1, u_2, u_3],
    )

    got = lax.all_to_all(pieces, ("yh", "yl"), 0, 0)
    pairs = [c for both in zip(c_own[:3], c_oth[:3]) for c in both]
    prods, cross = run(
        prods_kernel, "prods", [(unit, F32), ((2, 2, QC), F32)],
        [w_own] + pairs + c_own[3:] + c_oth[3:] + [qg, p, fac], 2300, 10, [((WIDTH, BLOCK), BF)],
        stack=tuple(range(1, 11)),
        picks={0: (lambda info, r: r.at[:, pl.ds(pl.multiple_of(info.x * 256, 256), 256)], (WIDTH, BLOCK))},
    )
    g_0, g_1, g_2, g_3, q_own, q_far = run(
        grads_kernel, "grads", [((2, TOK, BLOCK), BF)] * 4 + [((8, 16, BLOCK), BF)] * 2,
        [qg, p, fac, prods, cross, shift(cross, "yh", 1), pay], 270, 6, [((2, QC, BLOCK), F32)],
    )
    u_far = [shift(u_1, "x", 1), shift(u_2, "x", 2), shift(u_3, "x", -1)]
    z_in, q_own, *u_far = run(
        sum_y_kernel, "sum_y", [((8, 64, BLOCK), BF)], [got], 1, 2, ties=[q_own, *u_far], megabytes=60,
    )
    z_out = lax.all_to_all(z_in, "z", 0, 0)
    g_far = [shift(g_1, "x", 1), shift(g_2, "x", 2), shift(g_3, "x", -1)]
    joined, w_own, *g_far = run(
        join_kernel, "join", [((8, 24, BLOCK), F32)], [z_out, q_own, shift(q_far, "yh", 1)], 1, 1,
        ties=[w_own, *g_far],
    )
    keep, send = run(
        turn_kernel, "turn", [((8, TOK, BLOCK), BF)] * 2,
        [g_0, *g_far, u_0, *u_far], 1, 2,
    )
    got = shift(send, "k", 1)
    picks = {i: (lambda info, r: r.at[pl.ds(0, 4)], (4, TOK, BLOCK)) for i in range(2)}
    (key_grad,) = run(key_kernel, "key_home", [((TOK, WIDTH), BF)], [keep, got], 1, 2, picks=picks)

    joined = lax.all_to_all(joined, ring, 0, 0)
    picks = {i: (lambda info, r: r.at[pl.ds(4, 4)], (4, TOK, BLOCK)) for i in range(2)}
    (context_grad,) = run(
        context_kernel, "context_grad", [((TOK, WIDTH), BF)], [keep, got, w_own, shift(w_own, "k", 1)], 2200, 10,
        picks=picks,
    )
    weight_grad, query_grad = run(
        finish_kernel, "finish", [((8, WIDTH), F32), ((16, WIDTH), BF)], [joined, context_grad, key_grad], 1, 1,
        picks={i: (lambda info, r: r.at[pl.ds(0, 16), pl.ds(0, 128)], (16, 128)) for i in (1, 2)},
    )
    return (query_grad[None], key_grad[None], context_grad[None], weight_grad)


def solution(mesh):
    fine = Mesh(mesh.devices.reshape(2, 4, 2, 2, 8), AXES)
    fsdp = ("yl", "z")
    rows = P(fsdp, CTX, None)
    return jax.shard_map(
        on_device,
        mesh=fine,
        in_specs=(rows, rows, rows, rows, P(fsdp, None), P(fsdp, None, None), P(fsdp, None), P(fsdp, CTX)),
        out_specs=(rows, rows, rows, P(AXES, None)),
        check_vma=False,
    )
```

```python
import functools
import math

import jax
import jax.numpy as jnp
from jax import lax
from jax.experimental import pallas as pl
from jax.experimental.pallas import tpu as pltpu
from jax.sharding import Mesh, PartitionSpec as P

HD = 128
QC = 128
HEADS = 16
BLK = 64
TOK = 256
WIDTH = 2048
SCALE = 1.0 / math.sqrt(HD)
NEG = -1e30
BF = jnp.bfloat16
F32 = jnp.float32
CTX = ("yh", "x", "k")
AXES = ("yh", "x", "k", "yl", "z")
VMEM = pl.BlockSpec(memory_space=pltpu.VMEM)
SMEM = pl.BlockSpec(memory_space=pltpu.SMEM)

BLOCK = 256


def params(megabytes):
    return pltpu.CompilerParams(vmem_limit_bytes=megabytes << 20)


def cost(flops, size):
    return pl.CostEstimate(flops=flops, bytes_accessed=size, transcendentals=0)


def dot(a, b, ca, cb):
    return lax.dot_general(a, b, (((ca,), (cb,)), ((), ())), preferred_element_type=F32)


def shift(a, axis, by):
    n = lax.axis_size(axis)
    return lax.ppermute(a, axis, [(i, (i + by) % n) for i in range(n)])


class Info:
    def __init__(self, plan, lengths, blocks):
        self.x, self.k, self.yh, self.yl = (lax.axis_index(a) for a in ("x", "k", "yh", "yl"))
        self.start, self.width = plan[0, 0, 1], plan[0, 1, 1]
        self.lengths = [lengths[0, e] for e in range(2)]
        self.blocks = blocks


class Fetched:
    def __init__(self, src, dst, sem):
        self.copy = pltpu.make_async_copy(src, dst, sem)
        self.ref = dst
        self.copy.start()
        self.pending = True

    def __getitem__(self, at):
        self.ready()
        return self.ref[at]

    def ready(self):
        if self.pending:
            self.copy.wait()
            self.pending = False


def call(scalars, kernel, name, outs, args, flops, size, scratch=(), ties=(), picks=None, stack=(), megabytes=48):
    n_in, n_out, n_tie = len(args), len(outs), len(ties)
    picks = picks or {}
    plain = [i for i in range(n_in) if i not in stack]
    tall = sum(args[i].shape[0] for i in stack)

    def body(plan, lengths, blocks, *refs):
        info = Info(plan, lengths, blocks)
        srcs, refs = refs[:n_in], refs[n_in + n_tie :]
        out_refs, refs = refs[:n_out], refs[n_out + n_tie :]
        bufs, refs = dict(zip(plain, refs)), refs[len(plain) :]
        sems, rest = refs[0], refs[1:]
        at = 0
        for i in stack:
            bufs[i] = rest[0].at[pl.ds(at, args[i].shape[0])]
            at += args[i].shape[0]
        srcs = [picks[i][0](info, a) if i in picks else a for i, a in enumerate(srcs)]
        ins = [Fetched(a, bufs[i], sems.at[i]) for i, a in enumerate(srcs)]
        kernel(info, *ins, *out_refs, *rest)
        for a in ins:
            a.ready()

    anywhere = pl.BlockSpec(memory_space=pl.ANY)
    return pl.pallas_call(
        body,
        in_specs=[SMEM] * 3 + [anywhere] * (n_in + n_tie),
        out_specs=[VMEM] * n_out + [anywhere] * n_tie,
        out_shape=[jax.ShapeDtypeStruct(shape, kind) for shape, kind in outs]
        + [jax.ShapeDtypeStruct(a.shape, a.dtype) for a in ties],
        scratch_shapes=[
            pltpu.VMEM(picks[i][1] if i in picks else args[i].shape, args[i].dtype) for i in plain
        ]
        + [pltpu.SemaphoreType.DMA((n_in,))]
        + ([pltpu.VMEM((tall, args[stack[0]].shape[1]), args[stack[0]].dtype)] if stack else [])
        + [pltpu.VMEM(shape, kind) for shape, kind in scratch],
        input_output_aliases={3 + n_in + i: n_out + i for i in range(n_tie)},
        compiler_params=params(megabytes),
        cost_estimate=cost(1, 1),
        name=name,
    )(*scalars, *args, *ties)


def in_one(info, n):
    c = info.yh * 8 + n
    return (c >= info.start) & (c < info.start + info.width)


def pack_kernel(info, k_ref, q_ref, g_ref, w_ref, out_ref, w_out):
    for b in range(4):
        at = pl.ds(pl.multiple_of(b * 512 + info.k * 256, 256), 256)
        w_out[:, b * 256 : (b + 1) * 256] = w_ref[:, at]
    row = lax.broadcasted_iota(jnp.int32, (16, BLOCK), 0)
    held = jnp.zeros((16, BLOCK), F32)
    for slot in range(TOK // BLK):
        held = jnp.where(row == slot, info.blocks[0, slot].astype(F32), held)
    for j in range(8):
        cols = slice(j * BLOCK, (j + 1) * BLOCK)
        out_ref[j, 256:272, :] = q_ref[:, cols]
        out_ref[j, 272:288, :] = g_ref[:, cols]
        out_ref[j, 288:304, :] = held.astype(BF)
        out_ref[j, 0:256, :] = k_ref[:, cols]


def unpack_kernel(info, pay, out_ref):
    out_ref[...] = pay[...]


def scores_kernel(info, own, far, p_ref, top_ref, ex_ref, qg_ref):
    for which in range(2):
        for i in range(8):
            rows = slice(i * 16, (i + 1) * 16)
            qg_ref[which, info.yh, rows, :] = own[i, 256 + which * 16 : 272 + which * 16, :]
            qg_ref[which, 1 - info.yh, rows, :] = far[i, which * 16 : (which + 1) * 16, :]
    row = lax.broadcasted_iota(jnp.int32, (BLK, QC), 0).astype(F32)
    col = lax.broadcasted_iota(jnp.int32, (BLK, QC), 1).astype(F32)
    tops, sums, ones = [], [], []
    for n in range(8):
        one = in_one(info, n)
        e = one.astype(jnp.int32)
        length = jnp.where(one, info.lengths[1], info.lengths[0]).astype(F32)
        held = own[n, 288:304, 0:QC].astype(F32)
        masks = []
        for slot in range(TOK // BLK):
            b = held[slot : slot + 1, :]
            masks.append((b >= 0.0) & (b * BLK + row <= length - QC + col))
        visible = jnp.concatenate(masks, axis=0)
        top_rows, sum_rows = [], []
        for hh in range(2):
            hs = slice(hh * HD, (hh + 1) * HD)
            masked = jnp.where(visible, dot(own[n, 0:256, hs], qg_ref[0, e, :, hs], 1, 1) * SCALE, NEG)
            top = jnp.max(masked, axis=0, keepdims=True)
            p = jnp.where(visible, jnp.exp(masked - top), 0.0)
            p_ref[n, :, hs] = p.astype(BF)
            top_rows.append(top)
            sum_rows.append(jnp.sum(p, axis=0, keepdims=True))
        tops.append(jnp.concatenate(top_rows, axis=0))
        sums.append(jnp.concatenate(sum_rows, axis=0))
        ones.append(one)
        top_ref[n] = tops[n]
    for e in range(2):
        of_e = [one if e else jnp.logical_not(one) for one in ones]
        top = jnp.full((2, QC), NEG, F32)
        for n in range(8):
            top = jnp.maximum(top, jnp.where(of_e[n], tops[n], NEG))
        total = jnp.zeros((2, QC), F32)
        for n in range(8):
            total = total + jnp.where(of_e[n], sums[n] * jnp.exp(tops[n] - top), 0.0)
        ex_ref[0, e] = top
        ex_ref[1, e] = total


def probs_kernel(info, qg_ref, p_ref, top_ref, x0, x1, vg_ref, fac_ref):
    tops, invs = [], []
    for e in range(2):
        top = jnp.maximum(x0[0, e], x1[0, e])
        total = x0[1, e] * jnp.exp(x0[0, e] - top) + x1[1, e] * jnp.exp(x1[0, e] - top)
        tops.append(top)
        invs.append(1.0 / total)
    for n in range(8):
        one = in_one(info, n)
        e = one.astype(jnp.int32)
        factor = jnp.exp(top_ref[n] - jnp.where(one, tops[1], tops[0])) * jnp.where(one, invs[1], invs[0])
        fac_ref[n] = factor
        for hh in range(2):
            hs = slice(hh * HD, (hh + 1) * HD)
            pr = (p_ref[n, :, hs].astype(F32) * factor[hh : hh + 1, :]).astype(BF)
            vg_ref[n, :, hs] = dot(pr, qg_ref[1, e, :, hs], 1, 0).astype(BF)


def ring_index(info, step, other):
    return lax.rem(info.x + step, 4) * 2 + (1 - info.k if other else info.k)


def early_kernel(info, vg, a0, a1, a2, b0, b1, b2, out_ref, mark_ref):
    mark_ref[...] = jnp.zeros(mark_ref.shape, F32)
    for tile in range(8):
        cols = slice(tile * 256, (tile + 1) * 256)
        acc = jnp.zeros((256, BLOCK), F32)
        for other, refs in enumerate(((a0, a1, a2), (b0, b1, b2))):
            for step, c in zip((0, 3, 1), refs):
                acc = acc + dot(c[:, cols], vg[ring_index(info, step, other)], 0, 0)
        out_ref[cols, :] = acc


def late_kernel(info, acc_ref, vg, a_top, a_bot, b_top, b_bot, out_ref):
    for tile in range(8):
        cols = slice(tile * 256, (tile + 1) * 256)
        acc = acc_ref[cols, :]
        for other, (top, bot) in enumerate(((a_top, a_bot), (b_top, b_bot))):
            left = jnp.concatenate([top[:, cols], bot[:, cols]], axis=0)
            acc = acc + dot(left, vg[ring_index(info, 2, other)], 0, 0)
        for part in range(4):
            k, yl = part // 2, part % 2
            rows = acc[part * 64 : (part + 1) * 64].astype(BF)
            out_ref[(tile // 4) * 2 + yl, (tile % 4) * 2 + k] = rows


def sum_y_kernel(info, got_ref, out_ref):
    total = jnp.zeros((8, 8, 8, BLOCK), F32)
    for n in range(4):
        total = total + got_ref[n].astype(F32).reshape(8, 8, 8, BLOCK)
    for z in range(8):
        out_ref[z] = total[:, z].reshape(64, BLOCK).astype(BF)


def prods_kernel(info, w_ref, a0, b0, a1, b1, a2, b2, a3, a4, b3, b4, qg_ref, p_ref, fac_ref,
                 prod_ref, cross_ref, c_buf, v_buf):
    cross = [jnp.zeros((2, QC), F32) for _ in range(2)]
    for c in (a0, b0, a1, b1, a2, b2, a3, a4, b3, b4):
        c.ready()
    v_buf[...] = dot(c_buf[...], w_ref[...], 1, 0).astype(BF)
    turns = (
        (0, 0), (0, 1), (3, 0), (3, 1), (1, 0), (1, 1), (2, 0), (2, 1),
    )
    for at, (step, other) in enumerate(turns):
        n = ring_index(info, step, other)
        one = in_one(info, n)
        e = one.astype(jnp.int32)
        v = v_buf[at * TOK : (at + 1) * TOK, :]
        rows = []
        for hh in range(2):
            hs = slice(hh * HD, (hh + 1) * HD)
            prod = dot(v[:, hs], qg_ref[1, e, :, hs], 1, 1)
            prod_ref[n, :, hs] = prod
            pr = p_ref[n, :, hs].astype(F32) * fac_ref[n, hh : hh + 1, :]
            rows.append(jnp.sum(pr * prod, axis=0, keepdims=True))
        part = jnp.concatenate(rows, axis=0)
        cross[0] = cross[0] + jnp.where(one, 0.0, part)
        cross[1] = cross[1] + jnp.where(one, part, 0.0)
    for e in range(2):
        cross_ref[e] = cross[e]


def grads_kernel(info, qg_ref, p_ref, fac_ref, prod_ref, x0, x1, own, g0, g1, g2, g3, q_own, q_far, qp_buf):
    qp_buf[...] = jnp.zeros(qp_buf.shape, F32)
    deltas = [x0[e] + x1[e] for e in range(2)]
    for step, k in ((step, k) for step in range(4) for k in range(2)):
        n = lax.rem(info.x + step, 4) * 2 + k
        one = in_one(info, n)
        e = one.astype(jnp.int32)
        delta = jnp.where(one, deltas[1], deltas[0])
        for hh in range(2):
            hs = slice(hh * HD, (hh + 1) * HD)
            pr = p_ref[n, :, hs].astype(F32) * fac_ref[n, hh : hh + 1, :]
            ds = (pr * (prod_ref[n, :, hs] - delta[hh : hh + 1, :])).astype(BF)
            (g0, g1, g2, g3)[step][k, :, hs] = (SCALE * dot(ds, qg_ref[0, e, :, hs], 1, 0)).astype(BF)
            qp_buf[e, :, hs] += dot(ds, own[n, 0:256, hs], 0, 0)
    for out, e in ((q_own, info.yh), (q_far, 1 - info.yh)):
        out[...] = (SCALE * qp_buf[e]).astype(BF).reshape(8, 16, BLOCK)


def turn_kernel(info, g0, g1, g2, g3, keep_ref, send_ref):
    for step, g in enumerate((g0, g1, g2, g3)):
        keep_ref[step] = g[info.k]
        send_ref[step] = g[1 - info.k]


def key_kernel(info, keep, got, out_ref):
    for step in range(4):
        for other, part in enumerate((keep, got)):
            at = ring_index(info, 4 - step, other) * BLOCK
            out_ref[:, pl.ds(pl.multiple_of(at, BLOCK), BLOCK)] = part[step]


def join_kernel(info, got_ref, q0, q1, out_ref):
    total = jnp.zeros((64, BLOCK), F32)
    for n in range(8):
        total = total + got_ref[n].astype(F32)
    for j in range(8):
        out_ref[j, 0:8, :] = total[j * 8 : (j + 1) * 8]
        out_ref[j, 8:24, :] = q0[j].astype(F32) + q1[j].astype(F32)


def finish_kernel(info, got_ref, after, after_too, w_ref, q_ref):
    for j in range(8):
        cols = slice(j * BLOCK, (j + 1) * BLOCK)
        w_ref[:, cols] = got_ref[j, 0:8, :]
        q_ref[:, cols] = got_ref[j, 8:24, :].astype(BF)


def after_kernel(info, a, out_ref):
    out_ref[...] = a[...]


def context_kernel(info, home, w_own, w_oth, out_ref):
    left = [
        jnp.concatenate([home[b * 2 + k] for b in range(4)], axis=1) for k in (info.k, 1 - info.k)
    ]
    for t in range(4):
        rows = slice(t * 512, (t + 1) * 512)
        out_ref[:, rows] = (dot(left[0], w_own[rows, :], 1, 1) + dot(left[1], w_oth[rows, :], 1, 1)).astype(BF)


def halves_kernel(after, m1, p1, top_ref, bot_ref, m1_out, p1_out, top, bot, sems):
    copies = [
        pltpu.make_async_copy(m1.at[pl.ds(0, 128)], top, sems.at[0]),
        pltpu.make_async_copy(p1.at[pl.ds(128, 128)], bot, sems.at[1]),
    ]
    for c in copies:
        c.start()
    for c in copies:
        c.wait()
    top_ref[...] = top[...]
    bot_ref[...] = bot[...]


def on_device(queries, grad_out, keys, context, value_weight, plan, lengths, blocks):
    keys, context = keys[0], context[0]
    run = functools.partial(call, (plan, lengths, blocks))
    ring = ("x", "k")

    pay, w_own = run(
        pack_kernel, "pack", [((8, 304, BLOCK), BF), ((128, 1024), BF)],
        [keys, queries[0], grad_out[0], value_weight], 1, 3, megabytes=60,
    )
    w_own = lax.all_gather(w_own, ("yl", "z"), axis=0, tiled=True)
    pay = lax.all_to_all(pay, ring, 0, 0)
    (rows,) = run(
        unpack_kernel, "unpack", [((8, 32, BLOCK), BF)], [pay], 1, 1,
        picks={0: (lambda info, r: r.at[:, pl.ds(256, 32)], (8, 32, BLOCK))},
    )
    far = shift(rows, "yh", 1)

    c_m1, c_p1 = shift(context, "x", 1), shift(context, "x", -1)

    unit = (8, TOK, BLOCK)
    p, tops, ex, qg = run(
        scores_kernel, "scores",
        [(unit, BF), ((8, 2, QC), F32), ((2, 2, 2, QC), F32), ((2, 2, QC, BLOCK), BF)],
        [pay, far], 134, 4,
    )
    ex_far = shift(ex, "yh", 1)
    anywhere = pl.BlockSpec(memory_space=pl.ANY)
    half = jax.ShapeDtypeStruct((128, WIDTH), BF)
    whole = jax.ShapeDtypeStruct((TOK, WIDTH), BF)
    m1_top, p1_bot, c_m1, c_p1 = pl.pallas_call(
        halves_kernel,
        in_specs=[anywhere] * 3,
        out_specs=[VMEM, VMEM, anywhere, anywhere],
        out_shape=[half, half, whole, whole],
        scratch_shapes=[pltpu.VMEM((128, WIDTH), BF)] * 2 + [pltpu.SemaphoreType.DMA((2,))],
        input_output_aliases={1: 2, 2: 3},
        compiler_params=params(60),
        cost_estimate=cost(1, 1),
        name="halves",
    )(ex_far, c_m1, c_p1)
    c_own = [context, c_m1, c_p1, shift(m1_top, "x", 1), shift(p1_bot, "x", -1)]
    c_oth = [shift(c, "k", 1) for c in c_own[:3]]

    vg, fac = run(
        probs_kernel, "probs", [(unit, BF), ((8, 2, QC), F32)],
        [qg, p, tops, ex, ex_far], 134, 4,
    )
    home = lax.all_to_all(vg, ring, 0, 0)
    acc, mark = run(
        early_kernel, "block_early", [((WIDTH, BLOCK), F32), ((8, 128), F32)], [vg] + c_own[:3] + c_oth[:3], 1600, 8,
    )
    _, c_2a, c_2b = run(after_kernel, "after", [((8, 128), F32)], [mark], 1, 1, ties=c_own[3:])
    c_own[3:] = [c_2a, c_2b]
    c_oth = c_oth + [shift(c_2a, "k", 1), shift(c_2b, "k", 1)]
    (pieces,) = run(
        late_kernel, "block_late", [((4, 8, 64, BLOCK), BF)], [acc, vg] + c_own[3:] + c_oth[3:], 540, 4,
    )

    got = lax.all_to_all(pieces, ("yh", "yl"), 0, 0)
    pairs = [c for both in zip(c_own[:3], c_oth[:3]) for c in both]
    prods, cross, home = run(
        prods_kernel, "prods", [(unit, F32), ((2, 2, QC), F32)],
        [w_own] + pairs + c_own[3:] + c_oth[3:] + [qg, p, fac], 2300, 10, [((WIDTH, BLOCK), BF)],
        stack=tuple(range(1, 11)),
        picks={0: (lambda info, r: r.at[:, pl.ds(pl.multiple_of(info.x * 256, 256), 256)], (WIDTH, BLOCK))},
        ties=[home],
    )
    g_0, g_1, g_2, g_3, q_own, q_far = run(
        grads_kernel, "grads", [((2, TOK, BLOCK), BF)] * 4 + [((8, 16, BLOCK), BF)] * 2,
        [qg, p, fac, prods, cross, shift(cross, "yh", 1), pay], 270, 6, [((2, QC, BLOCK), F32)],
    )
    z_in, q_own = run(
        sum_y_kernel, "sum_y", [((8, 64, BLOCK), BF)], [got], 1, 2, ties=[q_own], megabytes=60,
    )
    z_out = lax.all_to_all(z_in, "z", 0, 0)
    g_far = [shift(g_1, "x", 1), shift(g_2, "x", 2), shift(g_3, "x", -1)]
    joined, w_own, *g_far = run(
        join_kernel, "join", [((8, 24, BLOCK), F32)], [z_out, q_own, shift(q_far, "yh", 1)], 1, 1,
        ties=[w_own, *g_far],
    )
    keep, send = run(
        turn_kernel, "turn", [((4, TOK, BLOCK), BF)] * 2,
        [g_0, *g_far], 1, 2,
    )
    (key_grad,) = run(key_kernel, "key_home", [((TOK, WIDTH), BF)], [keep, shift(send, "k", 1)], 1, 2)

    joined = lax.all_to_all(joined, ring, 0, 0)
    (context_grad,) = run(
        context_kernel, "context_grad", [((TOK, WIDTH), BF)], [home, w_own, shift(w_own, "k", 1)], 2200, 10,
    )
    weight_grad, query_grad = run(
        finish_kernel, "finish", [((8, WIDTH), F32), ((16, WIDTH), BF)], [joined, context_grad, key_grad], 1, 1,
        picks={i: (lambda info, r: r.at[pl.ds(0, 16), pl.ds(0, 128)], (16, 128)) for i in (1, 2)},
    )
    return (query_grad[None], key_grad[None], context_grad[None], weight_grad)


def solution(mesh):
    fine = Mesh(mesh.devices.reshape(2, 4, 2, 2, 8), AXES)
    fsdp = ("yl", "z")
    rows = P(fsdp, CTX, None)
    return jax.shard_map(
        on_device,
        mesh=fine,
        in_specs=(rows, rows, rows, rows, P(fsdp, None), P(fsdp, None, None), P(fsdp, None), P(fsdp, CTX)),
        out_specs=(rows, rows, rows, P(AXES, None)),
        check_vma=False,
    )
```

```python
import functools
import math

import jax
import jax.numpy as jnp
from jax import lax
from jax.experimental import pallas as pl
from jax.experimental.pallas import tpu as pltpu
from jax.sharding import Mesh, PartitionSpec as P

HD = 128
QC = 128
HEADS = 16
BLK = 64
TOK = 256
WIDTH = 2048
SCALE = 1.0 / math.sqrt(HD)
NEG = -1e30
BF = jnp.bfloat16
F32 = jnp.float32
CTX = ("yh", "x", "k")
AXES = ("yh", "x", "k", "yl", "z")
VMEM = pl.BlockSpec(memory_space=pltpu.VMEM)
SMEM = pl.BlockSpec(memory_space=pltpu.SMEM)

BLOCK = 256


def params(megabytes):
    return pltpu.CompilerParams(vmem_limit_bytes=megabytes << 20)


def cost(flops, size):
    return pl.CostEstimate(flops=flops, bytes_accessed=size, transcendentals=0)


def dot(a, b, ca, cb):
    return lax.dot_general(a, b, (((ca,), (cb,)), ((), ())), preferred_element_type=F32)


def shift(a, axis, by):
    n = lax.axis_size(axis)
    return lax.ppermute(a, axis, [(i, (i + by) % n) for i in range(n)])


class Info:
    def __init__(self, plan, lengths, blocks):
        self.x, self.k, self.yh, self.yl = (lax.axis_index(a) for a in ("x", "k", "yh", "yl"))
        self.start, self.width = plan[0, 0, 1], plan[0, 1, 1]
        self.lengths = [lengths[0, e] for e in range(2)]
        self.blocks = blocks


class Fetched:
    def __init__(self, src, dst, sem):
        self.copy = pltpu.make_async_copy(src, dst, sem)
        self.ref = dst
        self.copy.start()
        self.pending = True

    def __getitem__(self, at):
        self.ready()
        return self.ref[at]

    def ready(self):
        if self.pending:
            self.copy.wait()
            self.pending = False


def call(scalars, kernel, name, outs, args, flops, size, scratch=(), ties=(), picks=None, stack=(), megabytes=48):
    n_in, n_out, n_tie = len(args), len(outs), len(ties)
    picks = picks or {}
    plain = [i for i in range(n_in) if i not in stack]
    tall = sum(args[i].shape[0] for i in stack)

    def body(plan, lengths, blocks, *refs):
        info = Info(plan, lengths, blocks)
        srcs, refs = refs[:n_in], refs[n_in + n_tie :]
        out_refs, refs = refs[:n_out], refs[n_out + n_tie :]
        bufs, refs = dict(zip(plain, refs)), refs[len(plain) :]
        sems, rest = refs[0], refs[1:]
        at = 0
        for i in stack:
            bufs[i] = rest[0].at[pl.ds(at, args[i].shape[0])]
            at += args[i].shape[0]
        srcs = [picks[i][0](info, a) if i in picks else a for i, a in enumerate(srcs)]
        ins = [Fetched(a, bufs[i], sems.at[i]) for i, a in enumerate(srcs)]
        kernel(info, *ins, *out_refs, *rest)
        for a in ins:
            a.ready()

    anywhere = pl.BlockSpec(memory_space=pl.ANY)
    return pl.pallas_call(
        body,
        in_specs=[SMEM] * 3 + [anywhere] * (n_in + n_tie),
        out_specs=[VMEM] * n_out + [anywhere] * n_tie,
        out_shape=[jax.ShapeDtypeStruct(shape, kind) for shape, kind in outs]
        + [jax.ShapeDtypeStruct(a.shape, a.dtype) for a in ties],
        scratch_shapes=[
            pltpu.VMEM(picks[i][1] if i in picks else args[i].shape, args[i].dtype) for i in plain
        ]
        + [pltpu.SemaphoreType.DMA((n_in,))]
        + ([pltpu.VMEM((tall, args[stack[0]].shape[1]), args[stack[0]].dtype)] if stack else [])
        + [pltpu.VMEM(shape, kind) for shape, kind in scratch],
        input_output_aliases={3 + n_in + i: n_out + i for i in range(n_tie)},
        compiler_params=params(megabytes),
        cost_estimate=cost(1, 1),
        name=name,
    )(*scalars, *args, *ties)


def in_one(info, n):
    c = info.yh * 8 + n
    return (c >= info.start) & (c < info.start + info.width)


def pack_kernel(info, k_ref, q_ref, g_ref, w_ref, out_ref, w_out):
    for b in range(4):
        at = pl.ds(pl.multiple_of(b * 512 + info.k * 256, 256), 256)
        w_out[:, b * 256 : (b + 1) * 256] = w_ref[:, at]
    row = lax.broadcasted_iota(jnp.int32, (16, BLOCK), 0)
    held = jnp.zeros((16, BLOCK), F32)
    for slot in range(TOK // BLK):
        held = jnp.where(row == slot, info.blocks[0, slot].astype(F32), held)
    for j in range(8):
        cols = slice(j * BLOCK, (j + 1) * BLOCK)
        out_ref[j, 256:272, :] = q_ref[:, cols]
        out_ref[j, 272:288, :] = g_ref[:, cols]
        out_ref[j, 288:304, :] = held.astype(BF)
        out_ref[j, 0:256, :] = k_ref[:, cols]


def unpack_kernel(info, pay, out_ref):
    out_ref[...] = pay[...]


def scores_kernel(info, own, far, p_ref, top_ref, ex_ref, qg_ref):
    for which in range(2):
        for i in range(8):
            rows = slice(i * 16, (i + 1) * 16)
            qg_ref[which, info.yh, rows, :] = own[i, 256 + which * 16 : 272 + which * 16, :]
            qg_ref[which, 1 - info.yh, rows, :] = far[i, which * 16 : (which + 1) * 16, :]
    row = lax.broadcasted_iota(jnp.int32, (BLK, QC), 0).astype(F32)
    col = lax.broadcasted_iota(jnp.int32, (BLK, QC), 1).astype(F32)
    tops, sums, ones = [], [], []
    for n in range(8):
        one = in_one(info, n)
        e = one.astype(jnp.int32)
        length = jnp.where(one, info.lengths[1], info.lengths[0]).astype(F32)
        held = own[n, 288:304, 0:QC].astype(F32)
        masks = []
        for slot in range(TOK // BLK):
            b = held[slot : slot + 1, :]
            masks.append((b >= 0.0) & (b * BLK + row <= length - QC + col))
        visible = jnp.concatenate(masks, axis=0)
        top_rows, sum_rows = [], []
        for hh in range(2):
            hs = slice(hh * HD, (hh + 1) * HD)
            masked = jnp.where(visible, dot(own[n, 0:256, hs], qg_ref[0, e, :, hs], 1, 1) * SCALE, NEG)
            top = jnp.max(masked, axis=0, keepdims=True)
            p = jnp.where(visible, jnp.exp(masked - top), 0.0)
            p_ref[n, :, hs] = p.astype(BF)
            top_rows.append(top)
            sum_rows.append(jnp.sum(p, axis=0, keepdims=True))
        tops.append(jnp.concatenate(top_rows, axis=0))
        sums.append(jnp.concatenate(sum_rows, axis=0))
        ones.append(one)
        top_ref[n] = tops[n]
    for e in range(2):
        of_e = [one if e else jnp.logical_not(one) for one in ones]
        top = jnp.full((2, QC), NEG, F32)
        for n in range(8):
            top = jnp.maximum(top, jnp.where(of_e[n], tops[n], NEG))
        total = jnp.zeros((2, QC), F32)
        for n in range(8):
            total = total + jnp.where(of_e[n], sums[n] * jnp.exp(tops[n] - top), 0.0)
        ex_ref[0, e] = top
        ex_ref[1, e] = total


def probs_kernel(info, qg_ref, p_ref, top_ref, x0, x1, vg_ref, fac_ref):
    tops, invs = [], []
    for e in range(2):
        top = jnp.maximum(x0[0, e], x1[0, e])
        total = x0[1, e] * jnp.exp(x0[0, e] - top) + x1[1, e] * jnp.exp(x1[0, e] - top)
        tops.append(top)
        invs.append(1.0 / total)
    for n in range(8):
        one = in_one(info, n)
        e = one.astype(jnp.int32)
        factor = jnp.exp(top_ref[n] - jnp.where(one, tops[1], tops[0])) * jnp.where(one, invs[1], invs[0])
        fac_ref[n] = factor
        for hh in range(2):
            hs = slice(hh * HD, (hh + 1) * HD)
            pr = (p_ref[n, :, hs].astype(F32) * factor[hh : hh + 1, :]).astype(BF)
            vg_ref[n, :, hs] = dot(pr, qg_ref[1, e, :, hs], 1, 0).astype(BF)


def ring_index(info, step, other):
    return lax.rem(info.x + step, 4) * 2 + (1 - info.k if other else info.k)


def early_kernel(info, vg, a0, a1, a2, b0, b1, b2, out_ref, mark_ref):
    mark_ref[...] = jnp.zeros(mark_ref.shape, F32)
    for tile in range(8):
        cols = slice(tile * 256, (tile + 1) * 256)
        acc = jnp.zeros((256, BLOCK), F32)
        for other, refs in enumerate(((a0, a1, a2), (b0, b1, b2))):
            for step, c in zip((0, 3, 1), refs):
                acc = acc + dot(c[:, cols], vg[ring_index(info, step, other)], 0, 0)
        out_ref[cols, :] = acc


def late_kernel(info, acc_ref, vg, a_top, a_bot, b_top, b_bot, out_ref):
    for tile in range(8):
        cols = slice(tile * 256, (tile + 1) * 256)
        acc = acc_ref[cols, :]
        for other, (top, bot) in enumerate(((a_top, a_bot), (b_top, b_bot))):
            left = jnp.concatenate([top[:, cols], bot[:, cols]], axis=0)
            acc = acc + dot(left, vg[ring_index(info, 2, other)], 0, 0)
        for part in range(4):
            k, yl = part // 2, part % 2
            rows = acc[part * 64 : (part + 1) * 64].astype(BF)
            out_ref[(tile // 4) * 2 + yl, (tile % 4) * 2 + k] = rows


def sum_y_kernel(info, got_ref, out_ref):
    total = jnp.zeros((8, 8, 8, BLOCK), F32)
    for n in range(4):
        total = total + got_ref[n].astype(F32).reshape(8, 8, 8, BLOCK)
    for z in range(8):
        out_ref[z] = total[:, z].reshape(64, BLOCK).astype(BF)


def prods_kernel(info, w_ref, a0, b0, a1, b1, a2, b2, a3, a4, b3, b4, qg_ref, p_ref, fac_ref,
                 prod_ref, cross_ref, c_buf, v_buf):
    cross = [jnp.zeros((2, QC), F32) for _ in range(2)]
    for c in (a0, b0, a1, b1, a2, b2, a3, a4, b3, b4):
        c.ready()
    v_buf[...] = dot(c_buf[...], w_ref[...], 1, 0).astype(BF)
    turns = (
        (0, 0), (0, 1), (3, 0), (3, 1), (1, 0), (1, 1), (2, 0), (2, 1),
    )
    for at, (step, other) in enumerate(turns):
        n = ring_index(info, step, other)
        one = in_one(info, n)
        e = one.astype(jnp.int32)
        v = v_buf[at * TOK : (at + 1) * TOK, :]
        rows = []
        for hh in range(2):
            hs = slice(hh * HD, (hh + 1) * HD)
            prod = dot(v[:, hs], qg_ref[1, e, :, hs], 1, 1)
            prod_ref[n, :, hs] = prod
            pr = p_ref[n, :, hs].astype(F32) * fac_ref[n, hh : hh + 1, :]
            rows.append(jnp.sum(pr * prod, axis=0, keepdims=True))
        part = jnp.concatenate(rows, axis=0)
        cross[0] = cross[0] + jnp.where(one, 0.0, part)
        cross[1] = cross[1] + jnp.where(one, part, 0.0)
    for e in range(2):
        cross_ref[e] = cross[e]


def grads_kernel(info, qg_ref, p_ref, fac_ref, prod_ref, x0, x1, own, g0, g1, g2, g3, q_own, q_far, qp_buf):
    qp_buf[...] = jnp.zeros(qp_buf.shape, F32)
    deltas = [x0[e] + x1[e] for e in range(2)]
    for step, k in ((step, k) for step in range(4) for k in range(2)):
        n = lax.rem(info.x + step, 4) * 2 + k
        one = in_one(info, n)
        e = one.astype(jnp.int32)
        delta = jnp.where(one, deltas[1], deltas[0])
        for hh in range(2):
            hs = slice(hh * HD, (hh + 1) * HD)
            pr = p_ref[n, :, hs].astype(F32) * fac_ref[n, hh : hh + 1, :]
            ds = (pr * (prod_ref[n, :, hs] - delta[hh : hh + 1, :])).astype(BF)
            (g0, g1, g2, g3)[step][k, :, hs] = (SCALE * dot(ds, qg_ref[0, e, :, hs], 1, 0)).astype(BF)
            qp_buf[e, :, hs] += dot(ds, own[n, 0:256, hs], 0, 0)
    for out, e in ((q_own, info.yh), (q_far, 1 - info.yh)):
        out[...] = (SCALE * qp_buf[e]).astype(BF).reshape(8, 16, BLOCK)


def turn_kernel(info, g0, g1, g2, g3, keep_ref, send_ref):
    for step, g in enumerate((g0, g1, g2, g3)):
        keep_ref[step] = g[info.k]
        send_ref[step] = g[1 - info.k]


def key_kernel(info, keep, got, out_ref):
    for step in range(4):
        for other, part in enumerate((keep, got)):
            at = ring_index(info, 4 - step, other) * BLOCK
            out_ref[:, pl.ds(pl.multiple_of(at, BLOCK), BLOCK)] = part[step]


def join_kernel(info, got_ref, q0, q1, after, out_ref):
    total = jnp.zeros((64, BLOCK), F32)
    for n in range(8):
        total = total + got_ref[n].astype(F32)
    for j in range(8):
        out_ref[j, 0:8, :] = total[j * 8 : (j + 1) * 8]
        out_ref[j, 8:24, :] = q0[j].astype(F32) + q1[j].astype(F32)


def finish_kernel(info, got_ref, after, w_ref, q_ref):
    for j in range(8):
        cols = slice(j * BLOCK, (j + 1) * BLOCK)
        w_ref[:, cols] = got_ref[j, 0:8, :]
        q_ref[:, cols] = got_ref[j, 8:24, :].astype(BF)


def after_kernel(info, a, out_ref):
    out_ref[...] = a[...]


def context_kernel(info, home, w_own, w_oth, out_ref):
    left = [
        jnp.concatenate([home[b * 2 + k] for b in range(4)], axis=1) for k in (info.k, 1 - info.k)
    ]
    for t in range(4):
        rows = slice(t * 512, (t + 1) * 512)
        out_ref[:, rows] = (dot(left[0], w_own[rows, :], 1, 1) + dot(left[1], w_oth[rows, :], 1, 1)).astype(BF)


def halves_kernel(after, m1, p1, top_ref, bot_ref, m1_out, p1_out, top, bot, sems):
    copies = [
        pltpu.make_async_copy(m1.at[pl.ds(0, 128)], top, sems.at[0]),
        pltpu.make_async_copy(p1.at[pl.ds(128, 128)], bot, sems.at[1]),
    ]
    for c in copies:
        c.start()
    for c in copies:
        c.wait()
    top_ref[...] = top[...]
    bot_ref[...] = bot[...]


def on_device(queries, grad_out, keys, context, value_weight, plan, lengths, blocks):
    keys, context = keys[0], context[0]
    run = functools.partial(call, (plan, lengths, blocks))
    ring = ("x", "k")

    pay, w_own = run(
        pack_kernel, "pack", [((8, 304, BLOCK), BF), ((128, 1024), BF)],
        [keys, queries[0], grad_out[0], value_weight], 1, 3, megabytes=60,
    )
    w_own = lax.all_gather(w_own, ("yl", "z"), axis=0, tiled=True)
    pay = lax.all_to_all(pay, ring, 0, 0)
    (rows,) = run(
        unpack_kernel, "unpack", [((8, 32, BLOCK), BF)], [pay], 1, 1,
        picks={0: (lambda info, r: r.at[:, pl.ds(256, 32)], (8, 32, BLOCK))},
    )
    far = shift(rows, "yh", 1)

    c_m1, c_p1 = shift(context, "x", 1), shift(context, "x", -1)

    unit = (8, TOK, BLOCK)
    p, tops, ex, qg = run(
        scores_kernel, "scores",
        [(unit, BF), ((8, 2, QC), F32), ((2, 2, 2, QC), F32), ((2, 2, QC, BLOCK), BF)],
        [pay, far], 134, 4,
    )
    ex_far = shift(ex, "yh", 1)
    anywhere = pl.BlockSpec(memory_space=pl.ANY)
    half = jax.ShapeDtypeStruct((128, WIDTH), BF)
    whole = jax.ShapeDtypeStruct((TOK, WIDTH), BF)
    m1_top, p1_bot, c_m1, c_p1 = pl.pallas_call(
        halves_kernel,
        in_specs=[anywhere] * 3,
        out_specs=[VMEM, VMEM, anywhere, anywhere],
        out_shape=[half, half, whole, whole],
        scratch_shapes=[pltpu.VMEM((128, WIDTH), BF)] * 2 + [pltpu.SemaphoreType.DMA((2,))],
        input_output_aliases={1: 2, 2: 3},
        compiler_params=params(60),
        cost_estimate=cost(1, 1),
        name="halves",
    )(ex_far, c_m1, c_p1)
    c_own = [context, c_m1, c_p1, shift(m1_top, "x", 1), shift(p1_bot, "x", -1)]
    c_oth = [shift(c, "k", 1) for c in c_own[:3]]

    vg, fac = run(
        probs_kernel, "probs", [(unit, BF), ((8, 2, QC), F32)],
        [qg, p, tops, ex, ex_far], 134, 4,
    )
    home = lax.all_to_all(vg, ring, 0, 0)
    acc, mark = run(
        early_kernel, "block_early", [((WIDTH, BLOCK), F32), ((8, 128), F32)], [vg] + c_own[:3] + c_oth[:3], 1600, 8,
    )
    _, c_2a, c_2b = run(after_kernel, "after", [((8, 128), F32)], [mark], 1, 1, ties=c_own[3:])
    c_own[3:] = [c_2a, c_2b]
    c_oth = c_oth + [shift(c_2a, "k", 1), shift(c_2b, "k", 1)]
    (pieces,) = run(
        late_kernel, "block_late", [((4, 8, 64, BLOCK), BF)], [acc, vg] + c_own[3:] + c_oth[3:], 540, 4,
    )

    got = lax.all_to_all(pieces, ("yh", "yl"), 0, 0)
    pairs = [c for both in zip(c_own[:3], c_oth[:3]) for c in both]
    prods, cross, home = run(
        prods_kernel, "prods", [(unit, F32), ((2, 2, QC), F32)],
        [w_own] + pairs + c_own[3:] + c_oth[3:] + [qg, p, fac], 2300, 10, [((WIDTH, BLOCK), BF)],
        stack=tuple(range(1, 11)),
        picks={0: (lambda info, r: r.at[:, pl.ds(pl.multiple_of(info.x * 256, 256), 256)], (WIDTH, BLOCK))},
        ties=[home],
    )
    g_0, g_1, g_2, g_3, q_own, q_far = run(
        grads_kernel, "grads", [((2, TOK, BLOCK), BF)] * 4 + [((8, 16, BLOCK), BF)] * 2,
        [qg, p, fac, prods, cross, shift(cross, "yh", 1), pay], 270, 6, [((2, QC, BLOCK), F32)],
    )
    z_in, q_own, w_own = run(
        sum_y_kernel, "sum_y", [((8, 64, BLOCK), BF)], [got], 1, 2, ties=[q_own, w_own], megabytes=60,
    )
    z_out = lax.all_to_all(z_in, "z", 0, 0)
    g_far = [shift(g_1, "x", 1), shift(g_2, "x", 2), shift(g_3, "x", -1)]
    (context_grad,) = run(
        context_kernel, "context_grad", [((TOK, WIDTH), BF)], [home, w_own, shift(w_own, "k", 1)], 2200, 10,
    )
    joined, *g_far = run(
        join_kernel, "join", [((8, 24, BLOCK), F32)], [z_out, q_own, shift(q_far, "yh", 1), context_grad], 1, 1,
        ties=g_far, picks={3: (lambda info, r: r.at[pl.ds(0, 16), pl.ds(0, 128)], (16, 128))},
    )
    keep, send = run(
        turn_kernel, "turn", [((4, TOK, BLOCK), BF)] * 2,
        [g_0, *g_far], 1, 2,
    )
    (key_grad,) = run(key_kernel, "key_home", [((TOK, WIDTH), BF)], [keep, shift(send, "k", 1)], 1, 2)

    joined = lax.all_to_all(joined, ring, 0, 0)
    weight_grad, query_grad = run(
        finish_kernel, "finish", [((8, WIDTH), F32), ((16, WIDTH), BF)], [joined, key_grad], 1, 1,
        picks={1: (lambda info, r: r.at[pl.ds(0, 16), pl.ds(0, 128)], (16, 128))},
    )
    return (query_grad[None], key_grad[None], context_grad[None], weight_grad)


def solution(mesh):
    fine = Mesh(mesh.devices.reshape(2, 4, 2, 2, 8), AXES)
    fsdp = ("yl", "z")
    rows = P(fsdp, CTX, None)
    return jax.shard_map(
        on_device,
        mesh=fine,
        in_specs=(rows, rows, rows, rows, P(fsdp, None), P(fsdp, None, None), P(fsdp, None), P(fsdp, CTX)),
        out_specs=(rows, rows, rows, P(AXES, None)),
        check_vma=False,
    )
```
